32 devices in a mesh: atom: 8 (over z, core), energy: 4 (over y, x).
Axes of the slice: x: 2, y: 2, z: 4, core: 2. Of those that a mesh axis runs over, the one named last changes fastest.
Arguments:
- green: bfloat16 [64, 200, 512], P('atom', None, 'energy'), may hold values from -6 to 6
- coupling: bfloat16 [128, 800], P('atom'), may hold values from -0.625 to 0.625
- pairs: int32 [128, 2], P('atom'), may hold values from 0 to 63, as said below
- counts: int32 [8], P('atom'), may hold values from 8 to 16, as said below
- occupation: float32 [8], replicated, may hold values from 0.05 to 2
- offsets: int32 [8], replicated, may hold values from 1 to 64, as said below
Outputs:
- sigma: bfloat16 [64, 200, 512], P('atom', None, 'energy')
The draws below stay inside these ranges and needn't reach their ends.
Inputs may be any that keep to these rules, and one draw needn't show every extreme that they name: `pairs`: slot s lies in partition p = s // 16; its first atom is one of partition p, atoms p * 8 to (p + 1) * 8 - 1. Its second atom is another atom of partition p, or one of the first 2 atoms of partition p + 1 (then its first atom is one of the last 2 atoms of partition p), or one of the last 2 atoms of partition p - 1 (then its first atom is one of the first 2 atoms of partition p); in every partition that has such a neighbour some live slot bonds to the farthest of those 2 atoms. `counts`: some partition has all its slots live. `offsets`: some mode has the largest offset.
All inputs are finite; a program needn't handle non-finite values.
Results may differ from the reference program's by a relative error of at most 0.012.
Values may be sent and summed in bfloat16 or wider, within the bound.
A program may use at most 192 MiB of HBM per device.

```python
import math
import jax
import jax.numpy as jnp
from jax import lax

NORB = 10
MODES = 8
KMAX = 64
ATOM_DEV = 8
RIM = 2
PAIR_DEV = 16
PARTITIONS = 8
ATOMS = 64
PAIRS = 128
ENERGIES = 512


def draw_pairs(key, part):
    key = jax.random.fold_in(key, 11)
    keys = jax.random.split(key, 5)
    slots = jnp.arange(PAIRS, dtype=jnp.int32)
    owner = slots // PAIR_DEV
    within = slots % PAIR_DEV
    kind = jax.random.randint(keys[1], (PAIRS,), 0, 4)
    kind = jnp.where(within == 0, 2, kind)
    kind = jnp.where(within == 1, 3, kind)
    kind = jnp.where((kind == 2) & (owner == PARTITIONS - 1), 0, kind)
    kind = jnp.where((kind == 3) & (owner == 0), 0, kind)
    free_rel = jax.random.randint(keys[0], (PAIRS,), 0, ATOM_DEV)
    rim_rel = jax.random.randint(keys[4], (PAIRS,), 0, RIM)
    first_rel = jnp.where(kind == 2, ATOM_DEV - RIM + rim_rel, jnp.where(kind == 3, rim_rel, free_rel))
    depth = jax.random.randint(keys[2], (PAIRS,), 0, RIM)
    depth = jnp.where(within < 2, RIM - 1, depth)
    step_local = jax.random.randint(keys[3], (PAIRS,), 1, ATOM_DEV)
    local_rel = (first_rel + step_local) % ATOM_DEV
    second_rel = jnp.where(kind == 2, ATOM_DEV + depth, jnp.where(kind == 3, -1 - depth, local_rel))
    base = owner * ATOM_DEV
    return jnp.stack([base + first_rel, base + second_rel], axis=1).astype(jnp.int32)


def draw_counts(key, part):
    key = jax.random.fold_in(key, 23)
    keys = jax.random.split(key, 2)
    values = jax.random.randint(keys[0], (PARTITIONS,), PAIR_DEV // 2, PAIR_DEV + 1)
    place = jax.random.randint(keys[1], (), 0, PARTITIONS)
    return values.at[place].set(PAIR_DEV).astype(jnp.int32)


def draw_offsets(key, part):
    key = jax.random.fold_in(key, 37)
    keys = jax.random.split(key, 2)
    values = jax.random.randint(keys[0], (MODES,), 1, KMAX + 1)
    place = jax.random.randint(keys[1], (), 0, MODES)
    return values.at[place].set(KMAX).astype(jnp.int32)


def block_scale(stream_key, extent, cuts, smallest, top_value):
    def one(axis_at, blocks):
        heights = jax.random.uniform(jax.random.fold_in(jax.random.fold_in(stream_key, 6), axis_at), (blocks,), jnp.float32, smallest / len(cuts), top_value / len(cuts))
        return jnp.repeat(jnp.exp(heights), extent[axis_at] // blocks).reshape((-1,) + (1,) * (len(extent) - axis_at - 1))

    loudness = one(*cuts[0])
    for cut in cuts[1:]:
        loudness = loudness * one(*cut)
    return loudness


def centred(key, extent, scale, reach, pieces=(), kind=jnp.bfloat16):
    factor_of = block_scale(key, extent, pieces, -0.22, 0.18) if pieces else 1.0
    drawn = jax.random.normal(key, extent, jnp.float32) * scale * factor_of
    return jnp.minimum(jnp.maximum(drawn, -reach), reach).astype(kind)


def setup_inputs(seed: int = 0) -> dict:
    streams_of = jax.random.split(jax.random.key(seed), 7)
    return {
        "green": centred(streams_of[0], (ATOMS, 2 * NORB * NORB, ENERGIES), 1.0, 6.0, ((0, 8), (2, 4))),
        "coupling": centred(streams_of[1], (PAIRS, MODES * NORB * NORB), (8 * NORB) ** -0.5, 0.625, ((0, 8),)),
        "pairs": draw_pairs(jax.random.fold_in(streams_of[6], 71), 0),
        "counts": draw_counts(jax.random.fold_in(streams_of[6], 71), 0),
        "occupation": jnp.clip(jnp.exp(jax.random.uniform(streams_of[4], (MODES,), jnp.float32, math.log(0.05), math.log(2.0))), 0.05, 2.0),
        "offsets": draw_offsets(jax.random.fold_in(streams_of[6], 71), 0),
    }


def sandwich(blocks, weights, transpose):
    if transpose:
        inner = jnp.einsum("pji,prjke->prike", weights, blocks, precision=lax.Precision.HIGHEST)
        return jnp.einsum("prike,pkl->prile", inner, weights, precision=lax.Precision.HIGHEST)
    inner = jnp.einsum("pij,prjke->prike", weights, blocks, precision=lax.Precision.HIGHEST)
    return jnp.einsum("prike,plk->prile", inner, weights, precision=lax.Precision.HIGHEST)


def reference(green, coupling, pairs, counts, occupation, offsets):
    slab = 2 * NORB * NORB
    padded = jnp.pad(green, ((0, 0), (0, 0), (KMAX, KMAX)))
    slots = jnp.arange(PAIRS, dtype=jnp.int32)
    live = ((slots % PAIR_DEV) < counts[slots // PAIR_DEV]).astype(jnp.float32)
    block = math.gcd(PAIRS, 64)
    steps_count = PAIRS // block
    first_all = pairs[:, 0].reshape(steps_count, block)
    second_all = pairs[:, 1].reshape(steps_count, block)
    live_all = live.reshape(steps_count, block)
    coup_all = coupling.reshape(steps_count, block, MODES, NORB, NORB)

    def shifted_rows(rows, occ, step_size):
        lower = lax.dynamic_slice_in_dim(rows, (KMAX - step_size).astype(jnp.int32), ENERGIES, 2).astype(jnp.float32)
        upper = lax.dynamic_slice_in_dim(rows, (KMAX + step_size).astype(jnp.int32), ENERGIES, 2).astype(jnp.float32)
        mixed = (occ * lower + (occ + 1.0) * upper).astype(jnp.bfloat16)
        return mixed.astype(jnp.float32).reshape(block, 2, NORB, NORB, ENERGIES)

    def visit(total, items):
        first, second, mask, coup = items
        rows_a = padded[first]
        rows_b = padded[second]
        for mode in range(MODES):
            occ = occupation[mode]
            step_size = offsets[mode]
            weights = coup[:, mode].astype(jnp.float32)
            part_a = shifted_rows(rows_a, occ, step_size)
            part_b = shifted_rows(rows_b, occ, step_size)
            to_a = sandwich(part_b, weights, False) * mask[:, None, None, None, None]
            to_b = sandwich(part_a, weights, True) * mask[:, None, None, None, None]
            total = total.at[first].add(to_a.reshape(block, slab, ENERGIES))
            total = total.at[second].add(to_b.reshape(block, slab, ENERGIES))
        return total, None

    total = jnp.zeros((ATOMS, slab, ENERGIES), jnp.float32)
    total, _ = lax.scan(visit, total, (first_all, second_all, live_all, coup_all))
    return total.astype(jnp.bfloat16)
```

```python
import functools

import jax
import jax.numpy as jnp
import numpy as np
from jax import lax
from jax.experimental import pallas as pl
from jax.experimental.pallas import tpu as pltpu
from jax.sharding import PartitionSpec as P

NORB = 10
MODES = 8
KMAX = 64
SQ = NORB * NORB
PADROW = 16
KR = NORB * PADROW
ATOMS_DEV = 8
E_DEV = 128
SLOTS = 16
MESH = pl.DeviceIdType.MESH
F32 = jnp.float32
BF16 = jnp.bfloat16
UNROLL = 2


def expansion_tables():
    first = np.zeros((128, MODES * 128), np.float32)
    second = np.zeros((128, MODES * 128), np.float32)
    for m in range(MODES):
        for j in range(NORB):
            for k in range(NORB):
                col = m * 128 + j * NORB + k
                first[m * NORB + j, col] = 1
                second[m * NORB + k, col] = 1
    return first, second


def row_tables():
    spread = np.zeros((256, 2 * SQ), np.float32)
    collect = np.zeros((2 * SQ, 2 * KR), np.float32)
    for part in range(2):
        for r in range(SQ):
            spread[part * 128 + r, part * SQ + r] = 1
            collect[part * SQ + r, part * KR + (r // NORB) * PADROW + r % NORB] = 1
    return spread, collect


def exchange_kernel(na, ne, green, cct, meta, hl, hr, rc, rl, rr, cn, mn, to_r, to_l, rim_r, rim_l, send, recv):
    p = lax.axis_index("atom")
    q = lax.axis_index("energy")
    up, down = p < na - 1, p > 0
    right, left = q < ne - 1, q > 0
    where_to = {
        (0, 1): right,
        (0, -1): left,
        (1, 0): up,
        (-1, 0): down,
        (1, 1): up & right,
        (1, -1): up & left,
        (-1, 1): down & right,
        (-1, -1): down & left,
    }

    barrier = pltpu.get_barrier_semaphore()
    for (da, de), there in where_to.items():
        @pl.when(there)
        def _(da=da, de=de):
            pl.semaphore_signal(barrier, inc=1, device_id={"atom": p + da, "energy": q + de}, device_id_type=MESH)

    low = lax.broadcasted_iota(jnp.int32, (2 * SQ, E_DEV), 1) < 64

    def rolled(x):
        return pltpu.roll(x.astype(F32), 64, 1)

    def mix(a, b):
        return jnp.where(low, a, b).astype(BF16)

    for i in range(4):
        near = green[i].astype(F32)
        far = rolled(green[4 + i])
        to_r[i] = mix(far, near)
        to_l[i] = mix(near, far)
    six, seven = rolled(green[6]), green[7].astype(F32)
    rim_r[0] = mix(six, seven)
    rim_l[0] = mix(seven, six)
    zero, one = green[0].astype(F32), rolled(green[1])
    rim_r[1] = mix(one, zero)
    rim_l[1] = mix(zero, one)

    @pl.when(jnp.logical_not(left))
    def _():
        hl[...] = jnp.zeros_like(hl)
        rl[...] = jnp.zeros_like(rl)

    @pl.when(jnp.logical_not(right))
    def _():
        hr[...] = jnp.zeros_like(hr)
        rr[...] = jnp.zeros_like(rr)

    @pl.when(jnp.logical_not(down))
    def _():
        rc[0:2] = jnp.zeros((2,) + rc.shape[1:], BF16)
        cn[0] = jnp.zeros(cn.shape[1:], BF16)
        mn[0] = jnp.zeros(mn.shape[1:], jnp.int32)

        @pl.when(left)
        def _():
            rl[0] = jnp.zeros(rl.shape[1:], BF16)

        @pl.when(right)
        def _():
            rr[0] = jnp.zeros(rr.shape[1:], BF16)

    @pl.when(jnp.logical_not(up))
    def _():
        rc[2:4] = jnp.zeros((2,) + rc.shape[1:], BF16)
        cn[1] = jnp.zeros(cn.shape[1:], BF16)
        mn[1] = jnp.zeros(mn.shape[1:], jnp.int32)

        @pl.when(left)
        def _():
            rl[1] = jnp.zeros(rl.shape[1:], BF16)

        @pl.when(right)
        def _():
            rr[1] = jnp.zeros(rr.shape[1:], BF16)

    plan = [
        (to_r, hl, 0, 1),
        (to_l, hr, 0, -1),
        (rim_r.at[0], rl.at[0], 1, 1),
        (rim_l.at[0], rr.at[0], 1, -1),
        (rim_r.at[1], rl.at[1], -1, 1),
        (rim_l.at[1], rr.at[1], -1, -1),
        (green.at[pl.ds(6, 2)], rc.at[pl.ds(0, 2)], 1, 0),
        (green.at[pl.ds(0, 2)], rc.at[pl.ds(2, 2)], -1, 0),
        (cct, cn.at[0], 1, 0),
        (cct, cn.at[1], -1, 0),
        (meta, mn.at[0], 1, 0),
        (meta, mn.at[1], -1, 0),
    ]
    count = sum(there.astype(jnp.int32) for there in where_to.values())
    pl.semaphore_wait(barrier, count)
    copies = []
    for i, (src, dst, da, de) in enumerate(plan):
        copy = pltpu.make_async_remote_copy(
            src_ref=src,
            dst_ref=dst,
            send_sem=send.at[i],
            recv_sem=recv.at[i],
            device_id={"atom": p + da, "energy": q + de},
            device_id_type=MESH,
        )
        copies.append((copy, where_to[da, de], where_to[-da, -de]))
        pl.when(where_to[da, de])(copy.start)
    for copy, sends, gets in copies:
        pl.when(gets)(copy.wait_recv)
        pl.when(sends)(copy.wait_send)


def exchange(na, ne, green, cct, meta):
    vm = pl.BlockSpec(memory_space=pltpu.VMEM)
    slab = (2 * SQ, E_DEV)
    shape = jax.ShapeDtypeStruct
    return pl.pallas_call(
        functools.partial(exchange_kernel, na, ne),
        out_shape=[
            shape((4,) + slab, BF16),
            shape((4,) + slab, BF16),
            shape((4,) + slab, BF16),
            shape((2,) + slab, BF16),
            shape((2,) + slab, BF16),
            shape((2,) + cct.shape, BF16),
            shape((2,) + meta.shape, jnp.int32),
        ],
        in_specs=[vm] * 3,
        out_specs=[vm] * 7,
        scratch_shapes=[
            pltpu.VMEM((4,) + slab, BF16),
            pltpu.VMEM((4,) + slab, BF16),
            pltpu.VMEM((2,) + slab, BF16),
            pltpu.VMEM((2,) + slab, BF16),
            pltpu.SemaphoreType.DMA((12,)),
            pltpu.SemaphoreType.DMA((12,)),
        ],
        compiler_params=pltpu.CompilerParams(
            collective_id=0, has_side_effects=True, vmem_limit_bytes=24 * 2**20
        ),
        name="exchange",
    )(green, cct, meta)


def born_kernel(
    meta, mn, occupation, offsets, green, hl, hr, rc, rl, rr, ccc, cct, cn, first, second, spread, collect,
    out, ext, shifts, data, cc1, cc2, acc, kron, t_list, d_list, o_list,
):
    def place(rel):
        own = jnp.where(rel < 4, rel, rel + 2)
        below = jnp.where(rel == -2, 10, 4)
        above = jnp.where(rel == 8, 5, 11)
        return jnp.where(rel < 0, below, jnp.where(rel > 7, above, own))

    def append(n, keep, t, d, o):
        t_list[n] = t
        d_list[n] = d
        o_list[n] = o
        return n + keep.astype(jnp.int32)

    def listing(s, n):
        a, b = meta[0, s], meta[1, s]
        live = s < meta[2, 0]
        n = append(n, live, s, place(b), a)
        n = append(n, live & (b >= 0) & (b < 8), SLOTS + s, place(a), b)
        a, b = mn[0, 0, s] - 8, mn[0, 1, s] - 8
        n = append(n, (s < mn[0, 2, 0]) & (b >= 0) & (b < 8), 2 * SLOTS + s, place(a), b)
        a, b = mn[1, 0, s] + 8, mn[1, 1, s] + 8
        n = append(n, (s < mn[1, 2, 0]) & (b >= 0) & (b < 8), 3 * SLOTS + s, place(a), b)
        return n

    total = lax.fori_loop(0, SLOTS, listing, 0)
    for u in range(UNROLL):
        t_list[total + u] = 0
        d_list[total + u] = 0
        o_list[total + u] = ATOMS_DEV

    row = lax.broadcasted_iota(jnp.int32, (2 * E_DEV, E_DEV), 0)
    col = lax.broadcasted_iota(jnp.int32, (2 * E_DEV, E_DEV), 1)
    halo = row - E_DEV
    for kind in range(2):
        if kind == 0:
            energy = jnp.where(halo < 64, halo + 128, halo - 128)
        else:
            energy = jnp.where(halo < 64, halo - 64, halo + 64)
        delta = jnp.where(row < E_DEV, row, energy) - col
        for m in range(MODES):
            n, k = occupation[m], offsets[m]
            value = jnp.where(delta == -k, n, jnp.where(delta == k, n + 1.0, 0.0))
            shifts[kind, m // 2, :, (m % 2) * 128 : (m % 2) * 128 + 128] = value.astype(BF16)

    low = lax.broadcasted_iota(jnp.int32, (2 * SQ, E_DEV), 1) < 64

    def widen(d, centre, under, over):
        ext[d, :, 0:E_DEV] = centre
        ext[d, :, E_DEV:] = jnp.where(low, under.astype(F32), over.astype(F32)).astype(BF16)

    for i in range(4):
        widen(i, green[i], hr[i], hl[i])
        widen(6 + i, green[4 + i], hl[i], hr[i])
    widen(4, rc[1], rr[0], rl[0])
    widen(5, rc[2], rr[1], rl[1])
    widen(10, rc[0], rl[0], rr[0])
    widen(11, rc[3], rl[1], rr[1])

    def shift_atom(d, carry):
        kind = jnp.where(d < 6, 0, 1)
        rows = jnp.dot(spread[...], ext[d], preferred_element_type=F32).astype(BF16)
        for pair in range(MODES // 2):
            both = jnp.dot(rows, shifts[kind, pair], preferred_element_type=F32).astype(BF16)
            for half in range(2):
                at = (2 * pair + half) * 128
                for part in range(2):
                    data[d, at : at + 128, part * 128 : part * 128 + 128] = both[
                        part * 128 : part * 128 + 128, half * 128 : half * 128 + 128
                    ]
        return carry

    lax.fori_loop(0, ATOMS_DEV + 4, shift_atom, 0)

    for i, source in enumerate((ccc, cct, cn.at[0], cn.at[1])):
        rows = source[...].reshape(SLOTS * PADROW, 128)
        at = i * SLOTS * PADROW
        cc1[at : at + SLOTS * PADROW] = jnp.dot(rows, first[...], preferred_element_type=F32)
        cc2[at : at + SLOTS * PADROW] = jnp.dot(rows, second[...], preferred_element_type=F32)

    acc[...] = jnp.zeros_like(acc)

    def visit(step, carry):
        for u in range(UNROLL):
            at = step * UNROLL + u
            t, d, o = t_list[at], d_list[at], o_list[at]
            base = pl.multiple_of(t * PADROW, PADROW)
            right = cc2[pl.ds(base, PADROW), :]
            for i in range(NORB):
                left = cc1[pl.ds(base + i, 1), :]
                kron[u, i * PADROW : (i + 1) * PADROW, :] = (left * right).astype(BF16)
            acc[o] += jnp.dot(kron[u], data[d], preferred_element_type=F32)
        return carry

    lax.fori_loop(0, lax.div(total + UNROLL - 1, UNROLL), visit, 0)

    for o in range(ATOMS_DEV):
        mine = acc[o].astype(BF16)
        tall = jnp.concatenate([mine[:, :E_DEV], mine[:, E_DEV:]], axis=0)
        out[o] = jnp.dot(collect[...], tall, preferred_element_type=F32).astype(BF16)


def born(meta, mn, occupation, offsets, *arrays):
    vm = pl.BlockSpec(memory_space=pltpu.VMEM)
    sm = pl.BlockSpec(memory_space=pltpu.SMEM)
    rows = 4 * SLOTS * PADROW
    return pl.pallas_call(
        born_kernel,
        out_shape=jax.ShapeDtypeStruct((ATOMS_DEV, 2 * SQ, E_DEV), BF16),
        in_specs=[sm] * 4 + [vm] * len(arrays),
        out_specs=vm,
        scratch_shapes=[
            pltpu.VMEM((ATOMS_DEV + 4, 2 * SQ, 2 * E_DEV), BF16),
            pltpu.VMEM((2, MODES // 2, 2 * E_DEV, 256), BF16),
            pltpu.VMEM((ATOMS_DEV + 4, MODES * 128, 2 * E_DEV), BF16),
            pltpu.VMEM((rows, MODES * 128), F32),
            pltpu.VMEM((rows, MODES * 128), F32),
            pltpu.VMEM((ATOMS_DEV + 1, KR, 2 * E_DEV), F32),
            pltpu.VMEM((UNROLL, KR, MODES * 128), BF16),
            pltpu.SMEM((4 * SLOTS + UNROLL,), jnp.int32),
            pltpu.SMEM((4 * SLOTS + UNROLL,), jnp.int32),
            pltpu.SMEM((4 * SLOTS + UNROLL,), jnp.int32),
        ],
        compiler_params=pltpu.CompilerParams(vmem_limit_bytes=48 * 2**20),
        name="born",
    )(meta, mn, occupation, offsets, *arrays)


def per_device(na, ne, green, coupling, pairs, counts, occupation, offsets):
    base = lax.axis_index("atom") * ATOMS_DEV
    blocks = coupling.reshape(SLOTS, MODES, NORB, NORB)
    room = ((0, 0), (0, PADROW - NORB), (0, 128 - MODES * NORB))
    ccc = jnp.pad(blocks.transpose(0, 2, 1, 3).reshape(SLOTS, NORB, MODES * NORB), room)
    cct = jnp.pad(blocks.transpose(0, 3, 1, 2).reshape(SLOTS, NORB, MODES * NORB), room)
    rows = jnp.concatenate([(pairs - base).T, jnp.broadcast_to(counts, (1, SLOTS))], axis=0)
    meta = jnp.pad(rows, ((0, 5), (0, 128 - SLOTS)))
    hl, hr, rc, rl, rr, cn, mn = exchange(na, ne, green, cct, meta)
    tables = [jnp.asarray(table, BF16) for table in expansion_tables() + row_tables()]
    return born(meta, mn, occupation, offsets, green, hl, hr, rc, rl, rr, ccc, cct, cn, *tables)


def solution(mesh):
    placed = (P("atom", None, "energy"), P("atom", None), P("atom", None), P("atom"), P(), P())
    return jax.shard_map(
        functools.partial(per_device, mesh.shape["atom"], mesh.shape["energy"]),
        mesh=mesh,
        in_specs=placed,
        out_specs=P("atom", None, "energy"),
        check_vma=False,
    )
```

```python
import functools

import jax
import jax.numpy as jnp
import numpy as np
from jax import lax
from jax.experimental import pallas as pl
from jax.experimental.pallas import tpu as pltpu
from jax.sharding import PartitionSpec as P

NORB = 10
MODES = 8
KMAX = 64
SQ = NORB * NORB
PADROW = 16
KR = NORB * PADROW
ATOMS_DEV = 8
E_DEV = 128
SLOTS = 16
MESH = pl.DeviceIdType.MESH
F32 = jnp.float32
BF16 = jnp.bfloat16
UNROLL = 2


def expansion_tables():
    tables = np.zeros((4, SQ, NORB * 128), np.float32)
    for i in range(NORB):
        for j in range(NORB):
            for k in range(NORB):
                col = i * 128 + j * NORB + k
                tables[0, i * NORB + j, col] = 1
                tables[1, i * NORB + k, col] = 1
                tables[2, j * NORB + i, col] = 1
                tables[3, k * NORB + i, col] = 1
    return tables


def row_tables():
    spread = np.zeros((256, 2 * SQ), np.float32)
    collect = np.zeros((2 * SQ, 2 * KR), np.float32)
    for part in range(2):
        for r in range(SQ):
            spread[part * 128 + r, part * SQ + r] = 1
            collect[part * SQ + r, part * KR + (r // NORB) * PADROW + r % NORB] = 1
    return spread, collect


def exchange_kernel(
    na, ne, occupation, offsets, green, coupling, meta, tables, spread,
    data, left_cc, right_cc, mn,
    hl, hr, rc, rh, coup_n, to_r, to_l, forward, shifts, send, recv,
):
    p = lax.axis_index("atom")
    q = lax.axis_index("energy")
    up, down = p < na - 1, p > 0
    right, left = q < ne - 1, q > 0
    where_to = {(0, 1): right, (0, -1): left, (1, 0): up, (-1, 0): down}

    def peer(da, de):
        return {"atom": p + da, "energy": q + de}

    barrier = pltpu.get_barrier_semaphore()
    for (da, de), there in where_to.items():
        @pl.when(there)
        def _(da=da, de=de):
            pl.semaphore_signal(barrier, inc=1, device_id=peer(da, de), device_id_type=MESH)

    low = lax.broadcasted_iota(jnp.int32, (2 * SQ, E_DEV), 1) < 64

    def mix(a, b):
        return jnp.where(low, a, b).astype(BF16)

    def far_atom(c):
        return c + 6 if c < 2 else c + 2

    for c in range(4):
        near = green[c].astype(F32)
        far = pltpu.roll(green[far_atom(c)].astype(F32), 64, 1)
        to_r[c] = mix(far, near)
        to_l[c] = mix(near, far)

    def clear(ref):
        ref[...] = jnp.zeros(ref.shape, ref.dtype)

    @pl.when(jnp.logical_not(left))
    def _():
        clear(hl)

    @pl.when(jnp.logical_not(right))
    def _():
        clear(hr)

    for side, there in ((0, down), (1, up)):
        @pl.when(jnp.logical_not(there))
        def _(side=side):
            clear(rc.at[pl.ds(2 * side, 2)])
            clear(rh.at[pl.ds(2 * side, 2)])
            clear(coup_n.at[side])
            clear(mn.at[side])

    slots = iter(range(16))

    def copy_to(source, target, da, de):
        i = next(slots)
        copy = pltpu.make_async_remote_copy(
            src_ref=source,
            dst_ref=target,
            send_sem=send.at[i],
            recv_sem=recv.at[i],
            device_id=peer(da, de),
            device_id_type=MESH,
        )
        return copy, where_to[da, de], where_to[-da, -de]

    def start(items):
        for copy, sends, _ in items:
            pl.when(sends)(copy.start)

    def arrive(items):
        for copy, _, gets in items:
            pl.when(gets)(copy.wait_recv)

    def sent(items):
        for copy, sends, _ in items:
            pl.when(sends)(copy.wait_send)

    halos = [
        [copy_to(to_r.at[c], hl.at[c], 0, 1), copy_to(to_l.at[c], hr.at[c], 0, -1)] for c in range(4)
    ]
    small = [
        copy_to(coupling, coup_n.at[0], 1, 0),
        copy_to(coupling, coup_n.at[1], -1, 0),
        copy_to(meta, mn.at[0], 1, 0),
        copy_to(meta, mn.at[1], -1, 0),
    ]
    rims = [
        copy_to(green.at[pl.ds(6, 2)], rc.at[pl.ds(0, 2)], 1, 0),
        copy_to(green.at[pl.ds(0, 2)], rc.at[pl.ds(2, 2)], -1, 0),
    ]
    passed = [
        copy_to(forward.at[pl.ds(0, 2)], rh.at[pl.ds(0, 2)], 1, 0),
        copy_to(forward.at[pl.ds(2, 2)], rh.at[pl.ds(2, 2)], -1, 0),
    ]

    pl.semaphore_wait(barrier, sum(there.astype(jnp.int32) for there in where_to.values()))
    start(halos[0])
    start(halos[1])
    start(small)
    start(rims)
    start(halos[2])
    start(halos[3])

    row = lax.broadcasted_iota(jnp.int32, (2 * E_DEV, E_DEV), 0)
    col = lax.broadcasted_iota(jnp.int32, (2 * E_DEV, E_DEV), 1)
    outer = row - E_DEV
    for kind in range(2):
        if kind == 0:
            energy = jnp.where(outer < 64, outer + 128, outer - 128)
        else:
            energy = jnp.where(outer < 64, outer - 64, outer + 64)
        delta = jnp.where(row < E_DEV, row, energy) - col
        for m in range(MODES):
            n, k = occupation[m], offsets[m]
            value = jnp.where(delta == -k, n, jnp.where(delta == k, n + 1.0, 0.0))
            shifts[kind, m // 2, :, (m % 2) * 128 : (m % 2) * 128 + 128] = value.astype(BF16)

    def expand(source, table, target):
        rows = jnp.concatenate([source[:, m * SQ : (m + 1) * SQ] for m in range(MODES)], axis=0)
        wide = jnp.dot(rows, tables[table], preferred_element_type=F32)
        for m in range(MODES):
            for i in range(NORB):
                target[m, i * SLOTS : (i + 1) * SLOTS, :] = wide[
                    m * SLOTS : (m + 1) * SLOTS, i * 128 : (i + 1) * 128
                ]

    for group in range(4):
        right_cc[group, :, NORB * SLOTS :, :] = jnp.zeros((MODES, 256 - NORB * SLOTS, 128), F32)
    expand(coupling, 0, left_cc.at[0])
    expand(coupling, 1, right_cc.at[0])
    expand(coupling, 2, left_cc.at[1])
    expand(coupling, 3, right_cc.at[1])
    arrive(small)
    for side in range(2):
        expand(coup_n.at[side], 2, left_cc.at[2 + side])
        expand(coup_n.at[side], 3, right_cc.at[2 + side])

    def shift(d, kind, centre, halo):
        wide = jnp.concatenate([centre, halo], axis=1)
        rows = jnp.dot(spread[...], wide, preferred_element_type=F32).astype(BF16)
        for pair in range(MODES // 2):
            both = jnp.dot(rows, shifts[kind, pair], preferred_element_type=F32).astype(BF16)
            for half in range(2):
                at = (2 * pair + half) * 128
                for part in range(2):
                    data[d, at : at + 128, part * 128 : part * 128 + 128] = both[
                        part * 128 : part * 128 + 128, half * 128 : half * 128 + 128
                    ]

    def own_halos(c):
        lower, upper = hl[c].astype(F32), hr[c].astype(F32)
        return mix(upper, lower), mix(lower, upper)

    def shift_own(c, far):
        near_halo, far_halo = own_halos(c)
        shift(c, 0, green[c], near_halo)
        shift(6 + c, 1, green[far], far_halo)

    arrive(halos[0])
    arrive(halos[1])
    for c in range(2):
        near_halo, far_halo = own_halos(c)
        forward[c] = far_halo
        forward[2 + c] = near_halo
    start(passed)

    def first_half(c, carry):
        shift_own(c, c + 6)
        return carry

    lax.fori_loop(0, 2, first_half, 0)
    arrive(halos[2])
    shift_own(2, 4)
    arrive(rims)
    arrive(passed)

    def rim(c, carry):
        shift(4 + c, 0, rc[2 + c], rh[2 + c])
        shift(10 + c, 1, rc[c], rh[c])
        return carry

    lax.fori_loop(0, 2, rim, 0)
    arrive(halos[3])
    shift_own(3, 5)
    for items in halos + [small, rims, passed]:
        sent(items)


def exchange(na, ne, occupation, offsets, green, coupling, meta, tables, spread):
    vm = pl.BlockSpec(memory_space=pltpu.VMEM)
    sm = pl.BlockSpec(memory_space=pltpu.SMEM)
    slab = (2 * SQ, E_DEV)
    shape = jax.ShapeDtypeStruct
    return pl.pallas_call(
        functools.partial(exchange_kernel, na, ne),
        out_shape=[
            shape((ATOMS_DEV + 4, MODES * 128, 2 * E_DEV), BF16),
            shape((4, MODES, 256, 128), F32),
            shape((4, MODES, 256, 128), F32),
            shape((2,) + meta.shape, jnp.int32),
        ],
        in_specs=[sm] * 2 + [vm] * 5,
        out_specs=[vm] * 4,
        scratch_shapes=[
            pltpu.VMEM((4,) + slab, BF16),
            pltpu.VMEM((4,) + slab, BF16),
            pltpu.VMEM((4,) + slab, BF16),
            pltpu.VMEM((4,) + slab, BF16),
            pltpu.VMEM((2,) + coupling.shape, BF16),
            pltpu.VMEM((4,) + slab, BF16),
            pltpu.VMEM((4,) + slab, BF16),
            pltpu.VMEM((4,) + slab, BF16),
            pltpu.VMEM((2, MODES // 2, 2 * E_DEV, 256), BF16),
            pltpu.SemaphoreType.DMA((16,)),
            pltpu.SemaphoreType.DMA((16,)),
        ],
        compiler_params=pltpu.CompilerParams(
            collective_id=0, has_side_effects=True, vmem_limit_bytes=32 * 2**20
        ),
        name="exchange",
    )(occupation, offsets, green, coupling, meta, tables, spread)


def born_kernel(meta, mn, data, left_cc, right_cc, collect, out, acc, kron, t_list, d_list, o_list):
    base = lax.axis_index("atom") * ATOMS_DEV

    def place(rel):
        own = jnp.where((rel == 4) | (rel == 5), rel + 4, rel)
        return jnp.where(rel < 0, rel + 12, jnp.where(rel > 7, rel - 4, own))

    def append(n, keep, t, d, o):
        t_list[n] = t
        d_list[n] = d
        o_list[n] = o
        return n + keep.astype(jnp.int32)

    def listing(s, n):
        a, b = meta[0, s] - base, meta[1, s] - base
        live = s < meta[2, 0]
        n = append(n, live, s, place(b), a)
        n = append(n, live & (b >= 0) & (b < 8), SLOTS + s, place(a), b)
        for side in range(2):
            a, b = mn[side, 0, s] - base, mn[side, 1, s] - base
            live = (s < mn[side, 2, 0]) & (b >= 0) & (b < 8)
            n = append(n, live, (2 + side) * SLOTS + s, place(a), b)
        return n

    total = lax.fori_loop(0, SLOTS, listing, 0)
    for u in range(UNROLL):
        t_list[total + u] = 0
        d_list[total + u] = 0
        o_list[total + u] = ATOMS_DEV

    acc[...] = jnp.zeros_like(acc)

    def visit(step, carry):
        for u in range(UNROLL):
            at = step * UNROLL + u
            t, d, o = t_list[at], d_list[at], o_list[at]
            group, s = lax.shift_right_logical(t, 4), t & 15
            for m in range(MODES):
                right = right_cc[group, m, pl.ds(s, PADROW, stride=SLOTS), :]
                for i in range(NORB):
                    left = left_cc[group, m, pl.ds(i * SLOTS + s, 1), :]
                    kron[u, i * PADROW : (i + 1) * PADROW, m * 128 : (m + 1) * 128] = (left * right).astype(BF16)
            acc[o] += jnp.dot(kron[u], data[d], preferred_element_type=F32)
        return carry

    lax.fori_loop(0, lax.div(total + UNROLL - 1, UNROLL), visit, 0)

    for o in range(ATOMS_DEV):
        mine = acc[o].astype(BF16)
        tall = jnp.concatenate([mine[:, :E_DEV], mine[:, E_DEV:]], axis=0)
        out[o] = jnp.dot(collect[...], tall, preferred_element_type=F32).astype(BF16)


def born(meta, mn, *arrays):
    vm = pl.BlockSpec(memory_space=pltpu.VMEM)
    sm = pl.BlockSpec(memory_space=pltpu.SMEM)
    return pl.pallas_call(
        born_kernel,
        out_shape=jax.ShapeDtypeStruct((ATOMS_DEV, 2 * SQ, E_DEV), BF16),
        in_specs=[sm] * 2 + [vm] * len(arrays),
        out_specs=vm,
        scratch_shapes=[
            pltpu.VMEM((ATOMS_DEV + 1, KR, 2 * E_DEV), F32),
            pltpu.VMEM((UNROLL, KR, MODES * 128), BF16),
            pltpu.SMEM((4 * SLOTS + UNROLL,), jnp.int32),
            pltpu.SMEM((4 * SLOTS + UNROLL,), jnp.int32),
            pltpu.SMEM((4 * SLOTS + UNROLL,), jnp.int32),
        ],
        compiler_params=pltpu.CompilerParams(vmem_limit_bytes=32 * 2**20),
        name="born",
    )(meta, mn, *arrays)


def per_device(na, ne, green, coupling, pairs, counts, occupation, offsets):
    meta = jnp.concatenate([pairs.T, jnp.broadcast_to(counts, (1, SLOTS))], axis=0)
    spread, collect = row_tables()
    tables = jnp.asarray(expansion_tables(), BF16)
    data, left_cc, right_cc, mn = exchange(
        na, ne, occupation, offsets, green, coupling, meta, tables, jnp.asarray(spread, BF16)
    )
    return born(meta, mn, data, left_cc, right_cc, jnp.asarray(collect, BF16))


def solution(mesh):
    placed = (P("atom", None, "energy"), P("atom", None), P("atom", None), P("atom"), P(), P())
    return jax.shard_map(
        functools.partial(per_device, mesh.shape["atom"], mesh.shape["energy"]),
        mesh=mesh,
        in_specs=placed,
        out_specs=P("atom", None, "energy"),
        check_vma=False,
    )
```

```python
import functools

import jax
import jax.numpy as jnp
from jax import lax
from jax.experimental import pallas as pl
from jax.experimental.pallas import tpu as pltpu
from jax.sharding import PartitionSpec as P

NORB = 10
MODES = 8
KMAX = 64
SQ = NORB * NORB
PADROW = 16
KR = NORB * PADROW
ATOMS_DEV = 8
E_DEV = 128
SLOTS = 16
MESH = pl.DeviceIdType.MESH
F32 = jnp.float32
BF16 = jnp.bfloat16
UNROLL = 2


def fill_tables(tables):
    row = lax.broadcasted_iota(jnp.int32, (SQ, 128), 0)
    lane = lax.broadcasted_iota(jnp.int32, (SQ, 128), 1)
    j = lax.shift_right_logical(lane * 205, 11)
    k = lane - j * NORB
    inside = lane < SQ
    for i in range(NORB):
        for table, want in enumerate((i * NORB + j, i * NORB + k, j * NORB + i, k * NORB + i)):
            tables[table, :, i * 128 : (i + 1) * 128] = one_where(inside & (row == want))


def one_where(mask):
    return jnp.where(mask, 1.0, 0.0).astype(BF16)


def spread_matrix():
    row = lax.broadcasted_iota(jnp.int32, (256, 2 * SQ), 0)
    col = lax.broadcasted_iota(jnp.int32, (256, 2 * SQ), 1)
    first = (row < SQ) & (col == row)
    second = (row >= 128) & (row < 128 + SQ) & (col == row - 128 + SQ)
    return one_where(first | second)


def collect_matrix():
    row = lax.broadcasted_iota(jnp.int32, (2 * SQ, 2 * KR), 0)
    col = lax.broadcasted_iota(jnp.int32, (2 * SQ, 2 * KR), 1)
    part = jnp.where(col < KR, 0, 1)
    at = col - part * KR
    i, l = lax.shift_right_logical(at, 4), at & (PADROW - 1)
    return one_where((l < NORB) & (row == part * SQ + i * NORB + l))


def exchange_kernel(
    na, ne, green, pack,
    data, left_cc, right_cc, pack_n,
    hl, hr, rc, rh, to_r, to_l, forward, shifts, tables, spread, send, recv,
):
    p = lax.axis_index("atom")
    q = lax.axis_index("energy")
    up, down = p < na - 1, p > 0
    right, left = q < ne - 1, q > 0
    where_to = {(0, 1): right, (0, -1): left, (1, 0): up, (-1, 0): down}

    def peer(da, de):
        return {"atom": p + da, "energy": q + de}

    barrier = pltpu.get_barrier_semaphore()
    for (da, de), there in where_to.items():
        @pl.when(there)
        def _(da=da, de=de):
            pl.semaphore_signal(barrier, inc=1, device_id=peer(da, de), device_id_type=MESH)

    low = lax.broadcasted_iota(jnp.int32, (2 * SQ, E_DEV), 1) < 64

    def mix(a, b):
        return jnp.where(low, a, b).astype(BF16)

    def far_atom(c):
        return c + 6 if c < 2 else c + 2

    for c in range(4):
        near = green[c].astype(F32)
        far = pltpu.roll(green[far_atom(c)].astype(F32), 64, 1)
        to_r[c] = mix(far, near)
        to_l[c] = mix(near, far)

    def clear(ref):
        ref[...] = jnp.zeros(ref.shape, ref.dtype)

    @pl.when(jnp.logical_not(left))
    def _():
        clear(hl)

    @pl.when(jnp.logical_not(right))
    def _():
        clear(hr)

    for side, there in ((0, down), (1, up)):
        @pl.when(jnp.logical_not(there))
        def _(side=side):
            clear(rc.at[pl.ds(2 * side, 2)])
            clear(rh.at[pl.ds(2 * side, 2)])
            clear(pack_n.at[side])

    slots = iter(range(16))

    def copy_to(source, target, da, de):
        i = next(slots)
        copy = pltpu.make_async_remote_copy(
            src_ref=source,
            dst_ref=target,
            send_sem=send.at[i],
            recv_sem=recv.at[i],
            device_id=peer(da, de),
            device_id_type=MESH,
        )
        return copy, where_to[da, de], where_to[-da, -de]

    def start(items):
        for copy, sends, _ in items:
            pl.when(sends)(copy.start)

    def arrive(items):
        for copy, _, gets in items:
            pl.when(gets)(copy.wait_recv)

    def sent(items):
        for copy, sends, _ in items:
            pl.when(sends)(copy.wait_send)

    halos = [
        [copy_to(to_r.at[c], hl.at[c], 0, 1), copy_to(to_l.at[c], hr.at[c], 0, -1)] for c in range(4)
    ]
    small = [
        copy_to(pack, pack_n.at[0], 1, 0),
        copy_to(pack, pack_n.at[1], -1, 0),
    ]
    rims = [
        copy_to(green.at[pl.ds(6, 2)], rc.at[pl.ds(0, 2)], 1, 0),
        copy_to(green.at[pl.ds(0, 2)], rc.at[pl.ds(2, 2)], -1, 0),
    ]
    passed = [
        copy_to(forward.at[pl.ds(0, 2)], rh.at[pl.ds(0, 2)], 1, 0),
        copy_to(forward.at[pl.ds(2, 2)], rh.at[pl.ds(2, 2)], -1, 0),
    ]

    pl.semaphore_wait(barrier, sum(there.astype(jnp.int32) for there in where_to.values()))
    start(halos[0])
    start(halos[1])
    start(small)
    start(rims)
    start(halos[2])
    start(halos[3])

    row = lax.broadcasted_iota(jnp.int32, (2 * E_DEV, E_DEV), 0)
    col = lax.broadcasted_iota(jnp.int32, (2 * E_DEV, E_DEV), 1)
    outer = row - E_DEV
    for kind in range(2):
        if kind == 0:
            energy = jnp.where(outer < 64, outer + 128, outer - 128)
        else:
            energy = jnp.where(outer < 64, outer - 64, outer + 64)
        delta = (jnp.where(row < E_DEV, row, energy) - col).astype(F32)
        for m in range(MODES):
            n, k = pack[SLOTS + 3 : SLOTS + 4, m : m + 1], pack[SLOTS + 4 : SLOTS + 5, m : m + 1]
            value = jnp.where(delta == -k, n, jnp.where(delta == k, n + 1.0, 0.0))
            shifts[kind, m // 2, :, (m % 2) * 128 : (m % 2) * 128 + 128] = value.astype(BF16)

    def expand(source, table, target):
        rows = jnp.concatenate(
            [source[0:SLOTS, m * SQ : (m + 1) * SQ] for m in range(MODES)], axis=0
        ).astype(BF16)
        wide = jnp.dot(rows, tables[table], preferred_element_type=F32)
        for m in range(MODES):
            for i in range(NORB):
                target[m, i * SLOTS : (i + 1) * SLOTS, :] = wide[
                    m * SLOTS : (m + 1) * SLOTS, i * 128 : (i + 1) * 128
                ]

    for group in range(4):
        right_cc[group, :, NORB * SLOTS :, :] = jnp.zeros((MODES, 256 - NORB * SLOTS, 128), F32)
    fill_tables(tables)
    spread[...] = spread_matrix()
    expand(pack, 0, left_cc.at[0])
    expand(pack, 1, right_cc.at[0])
    expand(pack, 2, left_cc.at[1])
    expand(pack, 3, right_cc.at[1])
    arrive(small)
    for side in range(2):
        expand(pack_n.at[side], 2, left_cc.at[2 + side])
        expand(pack_n.at[side], 3, right_cc.at[2 + side])

    def shift(d, kind, centre, halo):
        wide = jnp.concatenate([centre, halo], axis=1)
        rows = jnp.dot(spread[...], wide, preferred_element_type=F32).astype(BF16)
        for pair in range(MODES // 2):
            both = jnp.dot(rows, shifts[kind, pair], preferred_element_type=F32).astype(BF16)
            for half in range(2):
                at = (2 * pair + half) * 128
                for part in range(2):
                    data[d, at : at + 128, part * 128 : part * 128 + 128] = both[
                        part * 128 : part * 128 + 128, half * 128 : half * 128 + 128
                    ]

    def own_halos(c):
        lower, upper = hl[c].astype(F32), hr[c].astype(F32)
        return mix(upper, lower), mix(lower, upper)

    def shift_own(c, far):
        near_halo, far_halo = own_halos(c)
        shift(c, 0, green[c], near_halo)
        shift(6 + c, 1, green[far], far_halo)

    arrive(halos[0])
    arrive(halos[1])
    for c in range(2):
        near_halo, far_halo = own_halos(c)
        forward[c] = far_halo
        forward[2 + c] = near_halo
    start(passed)

    def first_half(c, carry):
        shift_own(c, c + 6)
        return carry

    lax.fori_loop(0, 2, first_half, 0)
    arrive(halos[2])
    shift_own(2, 4)
    arrive(rims)
    arrive(passed)

    def rim(c, carry):
        shift(4 + c, 0, rc[2 + c], rh[2 + c])
        shift(10 + c, 1, rc[c], rh[c])
        return carry

    lax.fori_loop(0, 2, rim, 0)
    arrive(halos[3])
    shift_own(3, 5)
    for items in halos + [small, rims, passed]:
        sent(items)


def exchange(na, ne, green, pack):
    vm = pl.BlockSpec(memory_space=pltpu.VMEM)
    slab = (2 * SQ, E_DEV)
    shape = jax.ShapeDtypeStruct
    return pl.pallas_call(
        functools.partial(exchange_kernel, na, ne),
        out_shape=[
            shape((ATOMS_DEV + 4, MODES * 128, 2 * E_DEV), BF16),
            shape((4, MODES, 256, 128), F32),
            shape((4, MODES, 256, 128), F32),
            shape((2,) + pack.shape, F32),
        ],
        in_specs=[vm] * 2,
        out_specs=[vm] * 4,
        scratch_shapes=[
            pltpu.VMEM((4,) + slab, BF16),
            pltpu.VMEM((4,) + slab, BF16),
            pltpu.VMEM((4,) + slab, BF16),
            pltpu.VMEM((4,) + slab, BF16),
            pltpu.VMEM((4,) + slab, BF16),
            pltpu.VMEM((4,) + slab, BF16),
            pltpu.VMEM((4,) + slab, BF16),
            pltpu.VMEM((2, MODES // 2, 2 * E_DEV, 256), BF16),
            pltpu.VMEM((4, SQ, NORB * 128), BF16),
            pltpu.VMEM((256, 2 * SQ), BF16),
            pltpu.SemaphoreType.DMA((16,)),
            pltpu.SemaphoreType.DMA((16,)),
        ],
        compiler_params=pltpu.CompilerParams(
            collective_id=0, has_side_effects=True, vmem_limit_bytes=32 * 2**20
        ),
        name="exchange",
    )(green, pack)


def born_kernel(
    pack, pack_n, data, left_cc, right_cc, out, acc, kron, collect, lists, t_list, d_list, o_list, fetch
):
    fetches = [
        pltpu.make_async_copy(source.at[pl.ds(SLOTS, 8), pl.ds(0, 128)], lists.at[i], fetch.at[i])
        for i, source in enumerate((pack, pack_n.at[0], pack_n.at[1]))
    ]
    for one in fetches:
        one.start()
    collect[...] = collect_matrix()
    acc[...] = jnp.zeros_like(acc)
    for one in fetches:
        one.wait()

    def entry(source, r, s):
        return lists[source, r, s].astype(jnp.int32)

    base = lax.axis_index("atom") * ATOMS_DEV

    def place(rel):
        own = jnp.where((rel == 4) | (rel == 5), rel + 4, rel)
        return jnp.where(rel < 0, rel + 12, jnp.where(rel > 7, rel - 4, own))

    def append(n, keep, t, d, o):
        t_list[n] = t
        d_list[n] = d
        o_list[n] = o
        return n + keep.astype(jnp.int32)

    def listing(s, n):
        a, b = entry(0, 0, s) - base, entry(0, 1, s) - base
        live = s < entry(0, 2, 0)
        n = append(n, live, s, place(b), a)
        n = append(n, live & (b >= 0) & (b < 8), SLOTS + s, place(a), b)
        for side in range(2):
            a, b = entry(1 + side, 0, s) - base, entry(1 + side, 1, s) - base
            live = (s < entry(1 + side, 2, 0)) & (b >= 0) & (b < 8)
            n = append(n, live, (2 + side) * SLOTS + s, place(a), b)
        return n

    total = lax.fori_loop(0, SLOTS, listing, 0)
    for u in range(UNROLL + 1):
        t_list[total + u] = 0
        d_list[total + u] = 0
        o_list[total + u] = ATOMS_DEV

    def build(at, u):
        t = t_list[at]
        group, s = lax.shift_right_logical(t, 4), t & 15
        for m in range(MODES):
            right = right_cc[group, m, pl.ds(s, PADROW, stride=SLOTS), :]
            for i in range(NORB):
                left = left_cc[group, m, pl.ds(i * SLOTS + s, 1), :]
                kron[u, i * PADROW : (i + 1) * PADROW, m * 128 : (m + 1) * 128] = (left * right).astype(BF16)

    def visit(step, carry):
        for u in range(UNROLL):
            at = step * UNROLL + u
            d, o = d_list[at], o_list[at]
            term = jnp.dot(kron[u], data[d], preferred_element_type=F32)
            build(at + 1, (u + 1) % UNROLL)
            acc[o] += term
        return carry

    build(0, 0)
    lax.fori_loop(0, lax.div(total + UNROLL - 1, UNROLL), visit, 0)

    for o in range(ATOMS_DEV):
        mine = acc[o].astype(BF16)
        tall = jnp.concatenate([mine[:, :E_DEV], mine[:, E_DEV:]], axis=0)
        out[o] = jnp.dot(collect[...], tall, preferred_element_type=F32).astype(BF16)


def born(*arrays):
    vm = pl.BlockSpec(memory_space=pltpu.VMEM)
    return pl.pallas_call(
        born_kernel,
        out_shape=jax.ShapeDtypeStruct((ATOMS_DEV, 2 * SQ, E_DEV), BF16),
        in_specs=[vm] * len(arrays),
        out_specs=vm,
        scratch_shapes=[
            pltpu.VMEM((ATOMS_DEV + 1, KR, 2 * E_DEV), F32),
            pltpu.VMEM((UNROLL, KR, MODES * 128), BF16),
            pltpu.VMEM((2 * SQ, 2 * KR), BF16),
            pltpu.SMEM((3, 8, 128), F32),
            pltpu.SMEM((4 * SLOTS + UNROLL + 1,), jnp.int32),
            pltpu.SMEM((4 * SLOTS + UNROLL + 1,), jnp.int32),
            pltpu.SMEM((4 * SLOTS + UNROLL + 1,), jnp.int32),
            pltpu.SemaphoreType.DMA((3,)),
        ],
        compiler_params=pltpu.CompilerParams(vmem_limit_bytes=32 * 2**20),
        name="born",
    )(*arrays)


def per_device(na, ne, green, coupling, pairs, counts, occupation, offsets):
    def row(x):
        x = x.astype(F32).reshape(-1, x.shape[-1])
        return jnp.pad(x, ((0, 0), (0, coupling.shape[1] - x.shape[1])))

    pack = jnp.concatenate(
        [coupling.astype(F32), row(pairs.T), row(counts), row(occupation), row(offsets), jnp.zeros((3, coupling.shape[1]), F32)],
        axis=0,
    )
    data, left_cc, right_cc, pack_n = exchange(na, ne, green, pack)
    return born(pack, pack_n, data, left_cc, right_cc)


def solution(mesh):
    placed = (P("atom", None, "energy"), P("atom", None), P("atom", None), P("atom"), P(), P())
    return jax.shard_map(
        functools.partial(per_device, mesh.shape["atom"], mesh.shape["energy"]),
        mesh=mesh,
        in_specs=placed,
        out_specs=P("atom", None, "energy"),
        check_vma=False,
    )
```

```python
import functools

import jax
import jax.numpy as jnp
from jax import lax
from jax.experimental import pallas as pl
from jax.experimental.pallas import tpu as pltpu
from jax.sharding import PartitionSpec as P

NORB = 10
MODES = 8
KMAX = 64
SQ = NORB * NORB
PADROW = 16
KR = NORB * PADROW
ATOMS_DEV = 8
E_DEV = 128
SLOTS = 16
MESH = pl.DeviceIdType.MESH
F32 = jnp.float32
BF16 = jnp.bfloat16
UNROLL = 2


def fill_tables(tables):
    row = lax.broadcasted_iota(jnp.int32, (SQ, 128), 0)
    lane = lax.broadcasted_iota(jnp.int32, (SQ, 128), 1)
    j = lax.shift_right_logical(lane * 205, 11)
    k = lane - j * NORB
    inside = lane < SQ
    for i in range(NORB):
        for table, want in enumerate((i * NORB + j, i * NORB + k, j * NORB + i, k * NORB + i)):
            tables[table, :, i * 128 : (i + 1) * 128] = one_where(inside & (row == want))


def one_where(mask):
    return jnp.where(mask, 1.0, 0.0).astype(BF16)


def spread_matrix():
    row = lax.broadcasted_iota(jnp.int32, (256, 2 * SQ), 0)
    col = lax.broadcasted_iota(jnp.int32, (256, 2 * SQ), 1)
    first = (row < SQ) & (col == row)
    second = (row >= 128) & (row < 128 + SQ) & (col == row - 128 + SQ)
    return one_where(first | second)


def collect_matrix():
    row = lax.broadcasted_iota(jnp.int32, (2 * SQ, 2 * KR), 0)
    col = lax.broadcasted_iota(jnp.int32, (2 * SQ, 2 * KR), 1)
    part = jnp.where(col < KR, 0, 1)
    at = col - part * KR
    i, l = lax.shift_right_logical(at, 4), at & (PADROW - 1)
    return one_where((l < NORB) & (row == part * SQ + i * NORB + l))


def term_list(own, below, above, base):
    lane = lax.broadcasted_iota(jnp.int32, (1, 128), 1).astype(F32)

    def place(rel):
        inner = jnp.where((rel == 4) | (rel == 5), rel + 4, rel)
        return jnp.where(rel < 0, rel + 12, jnp.where(rel > 7, rel - 4, inner))

    entries = []
    for group, source in ((0, own), (2, below), (3, above)):
        a, b = source[0:1] - base, source[1:2] - base
        live = lane < source[2:3, 0:1]
        if group == 0:
            entries.append((live, lane, place(b), a))
            group = 1
        entries.append((live & (b >= 0) & (b < 8), group * SLOTS + lane, place(a), b))

    before = one_where(
        lax.broadcasted_iota(jnp.int32, (128, 128), 0) < lax.broadcasted_iota(jnp.int32, (128, 128), 1)
    )
    place_at = lax.broadcasted_iota(jnp.int32, (128, 128), 0).astype(F32)
    total = jnp.zeros((1, 1), F32)
    tables = [jnp.zeros((128, 128), F32) for _ in range(3)]
    for keep, *values in entries:
        flags = jnp.where(keep, 1.0, 0.0)
        many = jnp.broadcast_to(flags, (8, 128)).astype(BF16)
        at = jnp.dot(many, before, preferred_element_type=F32)[0:1] + total
        total = total + jnp.sum(flags, axis=1, keepdims=True)
        chosen = jnp.where(place_at == at, 1.0, 0.0) * flags
        tables = [table + chosen * value for table, value in zip(tables, values)]
    ones = jnp.ones((8, 128), BF16)
    t, d, o = (
        lax.dot_general(ones, table.astype(BF16), (((1,), (1,)), ((), ())), preferred_element_type=F32)
        for table in tables
    )
    row = lax.broadcasted_iota(jnp.int32, (8, 128), 0)
    index = lax.broadcasted_iota(jnp.int32, (8, 128), 1).astype(F32)
    o = jnp.where(index < total, o, float(ATOMS_DEV))
    out = jnp.where(row == 0, t, jnp.where(row == 1, d, jnp.where(row == 2, o, total)))
    return out.astype(jnp.int32)


def exchange_kernel(
    na, ne, green, pack,
    data, left_cc, right_cc, terms,
    pack_n, hl, hr, rc, rh, to_r, to_l, forward, shifts, tables, spread, send, recv,
):
    p = lax.axis_index("atom")
    q = lax.axis_index("energy")
    up, down = p < na - 1, p > 0
    right, left = q < ne - 1, q > 0
    where_to = {(0, 1): right, (0, -1): left, (1, 0): up, (-1, 0): down}

    def peer(da, de):
        return {"atom": p + da, "energy": q + de}

    barrier = pltpu.get_barrier_semaphore()
    for (da, de), there in where_to.items():
        @pl.when(there)
        def _(da=da, de=de):
            pl.semaphore_signal(barrier, inc=1, device_id=peer(da, de), device_id_type=MESH)

    low = lax.broadcasted_iota(jnp.int32, (2 * SQ, E_DEV), 1) < 64

    def mix(a, b):
        return jnp.where(low, a, b).astype(BF16)

    def far_atom(c):
        return c + 6 if c < 2 else c + 2

    for c in range(4):
        near = green[c].astype(F32)
        far = pltpu.roll(green[far_atom(c)].astype(F32), 64, 1)
        to_r[c] = mix(far, near)
        to_l[c] = mix(near, far)

    def clear(ref):
        ref[...] = jnp.zeros(ref.shape, ref.dtype)

    @pl.when(jnp.logical_not(left))
    def _():
        clear(hl)

    @pl.when(jnp.logical_not(right))
    def _():
        clear(hr)

    for side, there in ((0, down), (1, up)):
        @pl.when(jnp.logical_not(there))
        def _(side=side):
            clear(rc.at[pl.ds(2 * side, 2)])
            clear(rh.at[pl.ds(2 * side, 2)])
            clear(pack_n.at[side])

    slots = iter(range(16))

    def copy_to(source, target, da, de):
        i = next(slots)
        copy = pltpu.make_async_remote_copy(
            src_ref=source,
            dst_ref=target,
            send_sem=send.at[i],
            recv_sem=recv.at[i],
            device_id=peer(da, de),
            device_id_type=MESH,
        )
        return copy, where_to[da, de], where_to[-da, -de]

    def start(items):
        for copy, sends, _ in items:
            pl.when(sends)(copy.start)

    def arrive(items):
        for copy, _, gets in items:
            pl.when(gets)(copy.wait_recv)

    def sent(items):
        for copy, sends, _ in items:
            pl.when(sends)(copy.wait_send)

    halos = [
        [copy_to(to_r.at[c], hl.at[c], 0, 1), copy_to(to_l.at[c], hr.at[c], 0, -1)] for c in range(4)
    ]
    small = [
        copy_to(pack, pack_n.at[0], 1, 0),
        copy_to(pack, pack_n.at[1], -1, 0),
    ]
    rims = [
        copy_to(green.at[pl.ds(6, 2)], rc.at[pl.ds(0, 2)], 1, 0),
        copy_to(green.at[pl.ds(0, 2)], rc.at[pl.ds(2, 2)], -1, 0),
    ]
    passed = [
        copy_to(forward.at[pl.ds(0, 2)], rh.at[pl.ds(0, 2)], 1, 0),
        copy_to(forward.at[pl.ds(2, 2)], rh.at[pl.ds(2, 2)], -1, 0),
    ]

    pl.semaphore_wait(barrier, sum(there.astype(jnp.int32) for there in where_to.values()))
    start(halos[0])
    start(halos[1])
    start(small)
    start(rims)

    row = lax.broadcasted_iota(jnp.int32, (2 * E_DEV, E_DEV), 0)
    col = lax.broadcasted_iota(jnp.int32, (2 * E_DEV, E_DEV), 1)
    outer = row - E_DEV
    for kind in range(2):
        if kind == 0:
            energy = jnp.where(outer < 64, outer + 128, outer - 128)
        else:
            energy = jnp.where(outer < 64, outer - 64, outer + 64)
        delta = (jnp.where(row < E_DEV, row, energy) - col).astype(F32)
        for m in range(MODES):
            n, k = pack[SLOTS + 3 : SLOTS + 4, m : m + 1], pack[SLOTS + 4 : SLOTS + 5, m : m + 1]
            value = jnp.where(delta == -k, n, jnp.where(delta == k, n + 1.0, 0.0))
            shifts[kind, m // 2, :, (m % 2) * 128 : (m % 2) * 128 + 128] = value.astype(BF16)

    def expand(source, table, target):
        rows = jnp.concatenate(
            [source[0:SLOTS, m * SQ : (m + 1) * SQ] for m in range(MODES)], axis=0
        ).astype(BF16)
        wide = jnp.dot(rows, tables[table], preferred_element_type=F32)
        for m in range(MODES):
            for i in range(NORB):
                target[m, i * SLOTS : (i + 1) * SLOTS, :] = wide[
                    m * SLOTS : (m + 1) * SLOTS, i * 128 : (i + 1) * 128
                ]

    for group in range(4):
        right_cc[group, :, NORB * SLOTS :, :] = jnp.zeros((MODES, 256 - NORB * SLOTS, 128), F32)
    fill_tables(tables)
    spread[...] = spread_matrix()
    expand(pack, 0, left_cc.at[0])
    expand(pack, 1, right_cc.at[0])
    expand(pack, 2, left_cc.at[1])
    expand(pack, 3, right_cc.at[1])
    sent(halos[0])
    start(halos[2])
    arrive(small)
    for side in range(2):
        expand(pack_n.at[side], 2, left_cc.at[2 + side])
        expand(pack_n.at[side], 3, right_cc.at[2 + side])

    heads = [ref[SLOTS : SLOTS + 8, 0:128] for ref in (pack, pack_n.at[0], pack_n.at[1])]
    terms[...] = term_list(*heads, (p * ATOMS_DEV).astype(F32))

    def shift(d, kind, centre, halo):
        wide = jnp.concatenate([centre, halo], axis=1)
        rows = jnp.dot(spread[...], wide, preferred_element_type=F32).astype(BF16)
        for pair in range(MODES // 2):
            both = jnp.dot(rows, shifts[kind, pair], preferred_element_type=F32).astype(BF16)
            for half in range(2):
                at = (2 * pair + half) * 128
                for part in range(2):
                    data[d, at : at + 128, part * 128 : part * 128 + 128] = both[
                        part * 128 : part * 128 + 128, half * 128 : half * 128 + 128
                    ]

    def own_halos(c):
        lower, upper = hl[c].astype(F32), hr[c].astype(F32)
        return mix(upper, lower), mix(lower, upper)

    def shift_own(c, far):
        near_halo, far_halo = own_halos(c)
        shift(c, 0, green[c], near_halo)
        shift(6 + c, 1, green[far], far_halo)

    sent(halos[1])
    start(halos[3])
    arrive(halos[0])
    arrive(halos[1])
    for c in range(2):
        near_halo, far_halo = own_halos(c)
        forward[c] = far_halo
        forward[2 + c] = near_halo
    start(passed)

    def first_half(c, carry):
        shift_own(c, c + 6)
        return carry

    lax.fori_loop(0, 2, first_half, 0)
    arrive(halos[2])
    shift_own(2, 4)
    arrive(rims)
    arrive(passed)

    def rim(c, carry):
        shift(4 + c, 0, rc[2 + c], rh[2 + c])
        shift(10 + c, 1, rc[c], rh[c])
        return carry

    lax.fori_loop(0, 2, rim, 0)
    arrive(halos[3])
    shift_own(3, 5)
    for items in halos[2:] + [small, rims, passed]:
        sent(items)


def exchange(na, ne, green, pack):
    vm = pl.BlockSpec(memory_space=pltpu.VMEM)
    slab = (2 * SQ, E_DEV)
    shape = jax.ShapeDtypeStruct
    return pl.pallas_call(
        functools.partial(exchange_kernel, na, ne),
        out_shape=[
            shape((ATOMS_DEV + 4, MODES * 128, 2 * E_DEV), BF16),
            shape((4, MODES, 256, 128), F32),
            shape((4, MODES, 256, 128), F32),
            shape((8, 128), jnp.int32),
        ],
        in_specs=[vm] * 2,
        out_specs=[vm] * 4,
        scratch_shapes=[
            pltpu.VMEM((2,) + pack.shape, F32),
            pltpu.VMEM((4,) + slab, BF16),
            pltpu.VMEM((4,) + slab, BF16),
            pltpu.VMEM((4,) + slab, BF16),
            pltpu.VMEM((4,) + slab, BF16),
            pltpu.VMEM((4,) + slab, BF16),
            pltpu.VMEM((4,) + slab, BF16),
            pltpu.VMEM((4,) + slab, BF16),
            pltpu.VMEM((2, MODES // 2, 2 * E_DEV, 256), BF16),
            pltpu.VMEM((4, SQ, NORB * 128), BF16),
            pltpu.VMEM((256, 2 * SQ), BF16),
            pltpu.SemaphoreType.DMA((16,)),
            pltpu.SemaphoreType.DMA((16,)),
        ],
        compiler_params=pltpu.CompilerParams(
            collective_id=0, has_side_effects=True, vmem_limit_bytes=32 * 2**20
        ),
        name="exchange",
    )(green, pack)


def born_kernel(terms, data, left_cc, right_cc, out, acc, kron, collect):
    total = terms[3, 0]
    acc[...] = jnp.zeros_like(acc)

    def build(at, u):
        t = terms[0, at]
        group, s = lax.shift_right_logical(t, 4), t & 15
        for m in range(MODES):
            right = right_cc[group, m, pl.ds(s, PADROW, stride=SLOTS), :]
            for i in range(NORB):
                left = left_cc[group, m, pl.ds(i * SLOTS + s, 1), :]
                kron[u, i * PADROW : (i + 1) * PADROW, m * 128 : (m + 1) * 128] = (left * right).astype(BF16)

    def visit(step, carry):
        for u in range(UNROLL):
            at = step * UNROLL + u
            d, o = terms[1, at], terms[2, at]
            term = jnp.dot(kron[u], data[d], preferred_element_type=F32)
            build(at + 1, (u + 1) % UNROLL)
            acc[o] += term
        return carry

    build(0, 0)
    lax.fori_loop(0, lax.div(total + UNROLL - 1, UNROLL), visit, 0)

    collect[...] = collect_matrix()
    for o in range(0, ATOMS_DEV, 2):
        one, two = acc[o].astype(BF16), acc[o + 1].astype(BF16)
        tall = jnp.concatenate(
            [
                jnp.concatenate([one[:, :E_DEV], two[:, :E_DEV]], axis=1),
                jnp.concatenate([one[:, E_DEV:], two[:, E_DEV:]], axis=1),
            ],
            axis=0,
        )
        both = jnp.dot(collect[...], tall, preferred_element_type=F32).astype(BF16)
        out[o] = both[:, :E_DEV]
        out[o + 1] = both[:, E_DEV:]


def born(*arrays):
    vm = pl.BlockSpec(memory_space=pltpu.VMEM)
    return pl.pallas_call(
        born_kernel,
        out_shape=jax.ShapeDtypeStruct((ATOMS_DEV, 2 * SQ, E_DEV), BF16),
        in_specs=[pl.BlockSpec(memory_space=pltpu.SMEM)] + [vm] * 3,
        out_specs=vm,
        scratch_shapes=[
            pltpu.VMEM((ATOMS_DEV + 1, KR, 2 * E_DEV), F32),
            pltpu.VMEM((UNROLL, KR, MODES * 128), BF16),
            pltpu.VMEM((2 * SQ, 2 * KR), BF16),
        ],
        compiler_params=pltpu.CompilerParams(vmem_limit_bytes=32 * 2**20),
        name="born",
    )(*arrays)


def per_device(na, ne, green, coupling, pairs, counts, occupation, offsets):
    width = coupling.shape[1]
    row = lax.broadcasted_iota(jnp.int32, (SLOTS + 8, width), 0)
    pack = jnp.pad(coupling.astype(F32), ((0, 8), (0, 0)))
    for r, x in enumerate((pairs[:, 0], pairs[:, 1], counts, occupation, offsets)):
        line = jnp.pad(x.astype(F32), (0, width - x.shape[0]))
        pack = jnp.where(row == SLOTS + r, line[None, :], pack)
    data, left_cc, right_cc, terms = exchange(na, ne, green, pack)
    return born(terms, data, left_cc, right_cc)


def solution(mesh):
    placed = (P("atom", None, "energy"), P("atom", None), P("atom", None), P("atom"), P(), P())
    return jax.shard_map(
        functools.partial(per_device, mesh.shape["atom"], mesh.shape["energy"]),
        mesh=mesh,
        in_specs=placed,
        out_specs=P("atom", None, "energy"),
        check_vma=False,
    )
```

```python
import functools

import jax
import jax.numpy as jnp
from jax import lax
from jax.experimental import pallas as pl
from jax.experimental.pallas import tpu as pltpu
from jax.sharding import PartitionSpec as P

NORB = 10
MODES = 8
KMAX = 64
SQ = NORB * NORB
PADROW = 16
KR = NORB * PADROW
ATOMS_DEV = 8
E_DEV = 128
SLOTS = 16
MESH = pl.DeviceIdType.MESH
F32 = jnp.float32
BF16 = jnp.bfloat16
UNROLL = 4


def fill_tables(tables):
    row = lax.broadcasted_iota(jnp.int32, (SQ, 128), 0)
    lane = lax.broadcasted_iota(jnp.int32, (SQ, 128), 1)
    j = lax.shift_right_logical(lane * 205, 11)
    k = lane - j * NORB
    inside = lane < SQ
    for i in range(NORB):
        for table, want in enumerate((i * NORB + j, i * NORB + k, j * NORB + i, k * NORB + i)):
            tables[table, :, i * 128 : (i + 1) * 128] = one_where(inside & (row == want))


def one_where(mask):
    return jnp.where(mask, 1.0, 0.0).astype(BF16)


def spread_matrix():
    row = lax.broadcasted_iota(jnp.int32, (256, 2 * SQ), 0)
    col = lax.broadcasted_iota(jnp.int32, (256, 2 * SQ), 1)
    first = (row < SQ) & (col == row)
    second = (row >= 128) & (row < 128 + SQ) & (col == row - 128 + SQ)
    return one_where(first | second)


def collect_matrix():
    row = lax.broadcasted_iota(jnp.int32, (2 * SQ, 2 * KR), 0)
    col = lax.broadcasted_iota(jnp.int32, (2 * SQ, 2 * KR), 1)
    part = jnp.where(col < KR, 0, 1)
    at = col - part * KR
    i, l = lax.shift_right_logical(at, 4), at & (PADROW - 1)
    return one_where((l < NORB) & (row == part * SQ + i * NORB + l))


def term_list(own, below, above, base):
    lane = lax.broadcasted_iota(jnp.int32, (1, 128), 1).astype(F32)

    def place(rel):
        inner = jnp.where((rel == 4) | (rel == 5), rel + 4, rel)
        return jnp.where(rel < 0, rel + 12, jnp.where(rel > 7, rel - 4, inner))

    entries = []
    for group, source in ((0, own), (2, below), (3, above)):
        a, b = source[0:1] - base, source[1:2] - base
        live = lane < source[2:3, 0:1]
        if group == 0:
            entries.append((live, lane, place(b), a))
            group = 1
        entries.append((live & (b >= 0) & (b < 8), group * SLOTS + lane, place(a), b))

    before = one_where(
        lax.broadcasted_iota(jnp.int32, (128, 128), 0) < lax.broadcasted_iota(jnp.int32, (128, 128), 1)
    )
    place_at = lax.broadcasted_iota(jnp.int32, (128, 128), 0).astype(F32)
    total = jnp.zeros((1, 1), F32)
    tables = [jnp.zeros((128, 128), F32) for _ in range(3)]
    for keep, *values in entries:
        flags = jnp.where(keep, 1.0, 0.0)
        many = jnp.broadcast_to(flags, (8, 128)).astype(BF16)
        at = jnp.dot(many, before, preferred_element_type=F32)[0:1] + total
        total = total + jnp.sum(flags, axis=1, keepdims=True)
        chosen = jnp.where(place_at == at, 1.0, 0.0) * flags
        tables = [table + chosen * value for table, value in zip(tables, values)]
    ones = jnp.ones((8, 128), BF16)
    t, d, o = (
        lax.dot_general(ones, table.astype(BF16), (((1,), (1,)), ((), ())), preferred_element_type=F32)
        for table in tables
    )
    row = lax.broadcasted_iota(jnp.int32, (8, 128), 0)
    index = lax.broadcasted_iota(jnp.int32, (8, 128), 1).astype(F32)
    o = jnp.where(index < total, o, float(ATOMS_DEV))
    out = jnp.where(row == 0, t, jnp.where(row == 1, d, jnp.where(row == 2, o, total)))
    return out.astype(jnp.int32)


def exchange_kernel(
    na, ne, green, pack,
    data, kron, terms,
    left_cc, right_cc, pack_n, hl, hr, rc, rh, to_r, to_l, forward, shifts, tables, spread, send, recv,
):
    p = lax.axis_index("atom")
    q = lax.axis_index("energy")
    up, down = p < na - 1, p > 0
    right, left = q < ne - 1, q > 0
    where_to = {(0, 1): right, (0, -1): left, (1, 0): up, (-1, 0): down}

    def peer(da, de):
        return {"atom": p + da, "energy": q + de}

    barrier = pltpu.get_barrier_semaphore()
    for (da, de), there in where_to.items():
        @pl.when(there)
        def _(da=da, de=de):
            pl.semaphore_signal(barrier, inc=1, device_id=peer(da, de), device_id_type=MESH)

    low = lax.broadcasted_iota(jnp.int32, (2 * SQ, E_DEV), 1) < 64

    def mix(a, b):
        return jnp.where(low, a, b).astype(BF16)

    def far_atom(c):
        return c + 6 if c < 2 else c + 2

    for c in range(4):
        near = green[c].astype(F32)
        far = pltpu.roll(green[far_atom(c)].astype(F32), 64, 1)
        to_r[c] = mix(far, near)
        to_l[c] = mix(near, far)

    def clear(ref):
        ref[...] = jnp.zeros(ref.shape, ref.dtype)

    @pl.when(jnp.logical_not(left))
    def _():
        clear(hl)

    @pl.when(jnp.logical_not(right))
    def _():
        clear(hr)

    for side, there in ((0, down), (1, up)):
        @pl.when(jnp.logical_not(there))
        def _(side=side):
            clear(rc.at[pl.ds(2 * side, 2)])
            clear(rh.at[pl.ds(2 * side, 2)])
            clear(pack_n.at[side])

    slots = iter(range(16))

    def copy_to(source, target, da, de):
        i = next(slots)
        copy = pltpu.make_async_remote_copy(
            src_ref=source,
            dst_ref=target,
            send_sem=send.at[i],
            recv_sem=recv.at[i],
            device_id=peer(da, de),
            device_id_type=MESH,
        )
        return copy, where_to[da, de], where_to[-da, -de]

    def start(items):
        for copy, sends, _ in items:
            pl.when(sends)(copy.start)

    def arrive(items):
        for copy, _, gets in items:
            pl.when(gets)(copy.wait_recv)

    def sent(items):
        for copy, sends, _ in items:
            pl.when(sends)(copy.wait_send)

    halos = [
        [copy_to(to_r.at[c], hl.at[c], 0, 1), copy_to(to_l.at[c], hr.at[c], 0, -1)] for c in range(4)
    ]
    small = [
        copy_to(pack, pack_n.at[0], 1, 0),
        copy_to(pack, pack_n.at[1], -1, 0),
    ]
    rims = [
        copy_to(green.at[pl.ds(6, 2)], rc.at[pl.ds(0, 2)], 1, 0),
        copy_to(green.at[pl.ds(0, 2)], rc.at[pl.ds(2, 2)], -1, 0),
    ]
    passed = [
        copy_to(forward.at[pl.ds(0, 2)], rh.at[pl.ds(0, 2)], 1, 0),
        copy_to(forward.at[pl.ds(2, 2)], rh.at[pl.ds(2, 2)], -1, 0),
    ]

    pl.semaphore_wait(barrier, sum(there.astype(jnp.int32) for there in where_to.values()))
    start(halos[0])
    start(halos[1])
    start(small)
    start(rims)

    row = lax.broadcasted_iota(jnp.int32, (2 * E_DEV, E_DEV), 0)
    col = lax.broadcasted_iota(jnp.int32, (2 * E_DEV, E_DEV), 1)
    outer = row - E_DEV
    for kind in range(2):
        if kind == 0:
            energy = jnp.where(outer < 64, outer + 128, outer - 128)
        else:
            energy = jnp.where(outer < 64, outer - 64, outer + 64)
        delta = (jnp.where(row < E_DEV, row, energy) - col).astype(F32)
        for m in range(MODES):
            n, k = pack[SLOTS + 3 : SLOTS + 4, m : m + 1], pack[SLOTS + 4 : SLOTS + 5, m : m + 1]
            value = jnp.where(delta == -k, n, jnp.where(delta == k, n + 1.0, 0.0))
            shifts[kind, m // 2, :, (m % 2) * 128 : (m % 2) * 128 + 128] = value.astype(BF16)

    def expand(source, table, target):
        rows = jnp.concatenate(
            [source[0:SLOTS, m * SQ : (m + 1) * SQ] for m in range(MODES)], axis=0
        ).astype(BF16)
        wide = jnp.dot(rows, tables[table], preferred_element_type=F32)
        for m in range(MODES):
            for i in range(NORB):
                target[m, i * SLOTS : (i + 1) * SLOTS, :] = wide[
                    m * SLOTS : (m + 1) * SLOTS, i * 128 : (i + 1) * 128
                ]

    for group in range(4):
        right_cc[group, :, NORB * SLOTS :, :] = jnp.zeros((MODES, 256 - NORB * SLOTS, 128), F32)
    fill_tables(tables)
    spread[...] = spread_matrix()
    expand(pack, 0, left_cc.at[0])
    expand(pack, 1, right_cc.at[0])
    expand(pack, 2, left_cc.at[1])
    expand(pack, 3, right_cc.at[1])

    def build(group, s):
        for m in range(MODES):
            right = right_cc[group, m, pl.ds(s, PADROW, stride=SLOTS), :]
            for i in range(NORB):
                left = left_cc[group, m, pl.ds(i * SLOTS + s, 1), :]
                kron[group * SLOTS + s, i * PADROW : (i + 1) * PADROW, m * 128 : (m + 1) * 128] = (
                    left * right
                ).astype(BF16)

    def build_first(s, carry):
        build(0, s)
        return carry

    def build_second(s, carry):
        build(1, s)
        return carry

    def build_neighbours(s, carry):
        build(2, s)
        build(3, s)
        return carry

    lax.fori_loop(0, SLOTS, build_first, 0)
    sent(halos[0])
    start(halos[2])
    lax.fori_loop(0, SLOTS, build_second, 0)
    arrive(small)
    for side in range(2):
        expand(pack_n.at[side], 2, left_cc.at[2 + side])
        expand(pack_n.at[side], 3, right_cc.at[2 + side])

    heads = [ref[SLOTS : SLOTS + 8, 0:128] for ref in (pack, pack_n.at[0], pack_n.at[1])]
    terms[...] = term_list(*heads, (p * ATOMS_DEV).astype(F32))

    def shift(d, kind, centre, halo):
        wide = jnp.concatenate([centre, halo], axis=1)
        rows = jnp.dot(spread[...], wide, preferred_element_type=F32).astype(BF16)
        for pair in range(MODES // 2):
            both = jnp.dot(rows, shifts[kind, pair], preferred_element_type=F32).astype(BF16)
            for half in range(2):
                at = (2 * pair + half) * 128
                for part in range(2):
                    data[d, at : at + 128, part * 128 : part * 128 + 128] = both[
                        part * 128 : part * 128 + 128, half * 128 : half * 128 + 128
                    ]

    def own_halos(c):
        lower, upper = hl[c].astype(F32), hr[c].astype(F32)
        return mix(upper, lower), mix(lower, upper)

    def shift_own(c, far):
        near_halo, far_halo = own_halos(c)
        shift(c, 0, green[c], near_halo)
        shift(6 + c, 1, green[far], far_halo)

    sent(halos[1])
    start(halos[3])
    arrive(halos[0])
    arrive(halos[1])
    for c in range(2):
        near_halo, far_halo = own_halos(c)
        forward[c] = far_halo
        forward[2 + c] = near_halo
    start(passed)
    lax.fori_loop(0, SLOTS, build_neighbours, 0)

    def first_half(c, carry):
        shift_own(c, c + 6)
        return carry

    lax.fori_loop(0, 2, first_half, 0)
    arrive(halos[2])
    shift_own(2, 4)
    arrive(rims)
    arrive(passed)

    def rim(c, carry):
        shift(4 + c, 0, rc[2 + c], rh[2 + c])
        shift(10 + c, 1, rc[c], rh[c])
        return carry

    lax.fori_loop(0, 2, rim, 0)
    arrive(halos[3])
    shift_own(3, 5)
    for items in halos[2:] + [small, rims, passed]:
        sent(items)


def exchange(na, ne, green, pack):
    vm = pl.BlockSpec(memory_space=pltpu.VMEM)
    slab = (2 * SQ, E_DEV)
    shape = jax.ShapeDtypeStruct
    return pl.pallas_call(
        functools.partial(exchange_kernel, na, ne),
        out_shape=[
            shape((ATOMS_DEV + 4, MODES * 128, 2 * E_DEV), BF16),
            shape((4 * SLOTS, KR, MODES * 128), BF16),
            shape((8, 128), jnp.int32),
        ],
        in_specs=[vm] * 2,
        out_specs=[vm] * 3,
        scratch_shapes=[
            pltpu.VMEM((4, MODES, 256, 128), F32),
            pltpu.VMEM((4, MODES, 256, 128), F32),
            pltpu.VMEM((2,) + pack.shape, F32),
            pltpu.VMEM((4,) + slab, BF16),
            pltpu.VMEM((4,) + slab, BF16),
            pltpu.VMEM((4,) + slab, BF16),
            pltpu.VMEM((4,) + slab, BF16),
            pltpu.VMEM((4,) + slab, BF16),
            pltpu.VMEM((4,) + slab, BF16),
            pltpu.VMEM((4,) + slab, BF16),
            pltpu.VMEM((2, MODES // 2, 2 * E_DEV, 256), BF16),
            pltpu.VMEM((4, SQ, NORB * 128), BF16),
            pltpu.VMEM((256, 2 * SQ), BF16),
            pltpu.SemaphoreType.DMA((16,)),
            pltpu.SemaphoreType.DMA((16,)),
        ],
        compiler_params=pltpu.CompilerParams(
            collective_id=0, has_side_effects=True, vmem_limit_bytes=14 * 2**20
        ),
        name="exchange",
    )(green, pack)


def born_kernel(terms, data, kron, out, acc, collect):
    total = terms[3, 0]
    acc[...] = jnp.zeros_like(acc)

    def visit(step, carry):
        for u in range(UNROLL):
            at = step * UNROLL + u
            t, d, o = terms[0, at], terms[1, at], terms[2, at]
            acc[o] += jnp.dot(kron[t], data[d], preferred_element_type=F32)
        return carry

    lax.fori_loop(0, lax.div(total + UNROLL - 1, UNROLL), visit, 0)

    collect[...] = collect_matrix()
    for o in range(0, ATOMS_DEV, 2):
        one, two = acc[o].astype(BF16), acc[o + 1].astype(BF16)
        tall = jnp.concatenate(
            [
                jnp.concatenate([one[:, :E_DEV], two[:, :E_DEV]], axis=1),
                jnp.concatenate([one[:, E_DEV:], two[:, E_DEV:]], axis=1),
            ],
            axis=0,
        )
        both = jnp.dot(collect[...], tall, preferred_element_type=F32).astype(BF16)
        out[o] = both[:, :E_DEV]
        out[o + 1] = both[:, E_DEV:]


def born(*arrays):
    vm = pl.BlockSpec(memory_space=pltpu.VMEM)
    return pl.pallas_call(
        born_kernel,
        out_shape=jax.ShapeDtypeStruct((ATOMS_DEV, 2 * SQ, E_DEV), BF16),
        in_specs=[pl.BlockSpec(memory_space=pltpu.SMEM)] + [vm] * 2,
        out_specs=vm,
        scratch_shapes=[
            pltpu.VMEM((ATOMS_DEV + 1, KR, 2 * E_DEV), F32),
            pltpu.VMEM((2 * SQ, 2 * KR), BF16),
        ],
        compiler_params=pltpu.CompilerParams(vmem_limit_bytes=6 * 2**20),
        name="born",
    )(*arrays)


def per_device(na, ne, green, coupling, pairs, counts, occupation, offsets):
    width = coupling.shape[1]
    row = lax.broadcasted_iota(jnp.int32, (SLOTS + 8, width), 0)
    pack = jnp.pad(coupling.astype(F32), ((0, 8), (0, 0)))
    for r, x in enumerate((pairs[:, 0], pairs[:, 1], counts, occupation, offsets)):
        line = jnp.pad(x.astype(F32), (0, width - x.shape[0]))
        pack = jnp.where(row == SLOTS + r, line[None, :], pack)
    data, kron, terms = exchange(na, ne, green, pack)
    return born(terms, data, kron)


def solution(mesh):
    placed = (P("atom", None, "energy"), P("atom", None), P("atom", None), P("atom"), P(), P())
    return jax.shard_map(
        functools.partial(per_device, mesh.shape["atom"], mesh.shape["energy"]),
        mesh=mesh,
        in_specs=placed,
        out_specs=P("atom", None, "energy"),
        check_vma=False,
    )
```

```python
import functools

import jax
import jax.numpy as jnp
from jax import lax
from jax.experimental import pallas as pl
from jax.experimental.pallas import tpu as pltpu
from jax.sharding import PartitionSpec as P

NORB = 10
MODES = 8
KMAX = 64
SQ = NORB * NORB
PADROW = 16
KR = NORB * 8 + 2 * PADROW
ATOMS_DEV = 8
E_DEV = 128
SLOTS = 16
MESH = pl.DeviceIdType.MESH
F32 = jnp.float32
BF16 = jnp.bfloat16
UNROLL = 4


def fill_tables(tables):
    row = lax.broadcasted_iota(jnp.int32, (SQ, 128), 0)
    lane = lax.broadcasted_iota(jnp.int32, (SQ, 128), 1)
    j = lax.shift_right_logical(lane * 205, 11)
    k = lane - j * NORB
    inside = lane < SQ
    for i in range(NORB):
        for table, want in enumerate((i * NORB + j, i * NORB + k, j * NORB + i, k * NORB + i)):
            tables[table, :, i * 128 : (i + 1) * 128] = one_where(inside & (row == want))


def one_where(mask):
    return jnp.where(mask, 1.0, 0.0).astype(BF16)


def spread_matrix():
    row = lax.broadcasted_iota(jnp.int32, (256, 2 * SQ), 0)
    col = lax.broadcasted_iota(jnp.int32, (256, 2 * SQ), 1)
    first = (row < SQ) & (col == row)
    second = (row >= 128) & (row < 128 + SQ) & (col == row - 128 + SQ)
    return one_where(first | second)


def collect_matrix():
    row = lax.broadcasted_iota(jnp.int32, (2 * SQ, 2 * KR), 0)
    col = lax.broadcasted_iota(jnp.int32, (2 * SQ, 2 * KR), 1)
    part = jnp.where(col < KR, 0, 1)
    at = col - part * KR
    late = at - NORB * 8
    early = late < 0
    i = jnp.where(early, lax.shift_right_logical(at, 3), late & (PADROW - 1))
    l = jnp.where(early, at & 7, 8 + lax.shift_right_logical(jnp.maximum(late, 0), 4))
    return one_where((i < NORB) & (row == part * SQ + i * NORB + l))


def term_list(own, below, above, base):
    lane = lax.broadcasted_iota(jnp.int32, (1, SLOTS), 1).astype(F32)

    def place(rel):
        inner = jnp.where((rel == 4) | (rel == 5), rel + 4, rel)
        return jnp.where(rel < 0, rel + 12, jnp.where(rel > 7, rel - 4, inner))

    entries = []
    for group, source in ((0, own), (2, below), (3, above)):
        a, b = source[0:1].astype(F32) - base, source[1:2].astype(F32) - base
        live = lane < source[2:3].astype(F32)
        if group == 0:
            entries.append((live, lane, place(b), a))
            group = 1
        entries.append((live & (b >= 0) & (b < 8), group * SLOTS + lane, place(a), b))

    before = one_where(
        lax.broadcasted_iota(jnp.int32, (SLOTS, SLOTS), 0) < lax.broadcasted_iota(jnp.int32, (SLOTS, SLOTS), 1)
    )
    place_at = lax.broadcasted_iota(jnp.int32, (128, SLOTS), 0).astype(F32)
    total = jnp.zeros((1, 1), F32)
    tables = [jnp.zeros((128, SLOTS), F32) for _ in range(3)]
    for keep, *values in entries:
        flags = jnp.where(keep, 1.0, 0.0)
        many = jnp.broadcast_to(flags, (8, SLOTS)).astype(BF16)
        at = jnp.dot(many, before, preferred_element_type=F32)[0:1] + total
        total = total + jnp.sum(flags, axis=1, keepdims=True)
        chosen = jnp.where(place_at == at, 1.0, 0.0) * flags
        tables = [table + chosen * value for table, value in zip(tables, values)]
    ones = jnp.ones((8, SLOTS), BF16)
    t, d, o = (
        lax.dot_general(ones, table.astype(BF16), (((1,), (1,)), ((), ())), preferred_element_type=F32)
        for table in tables
    )
    row = lax.broadcasted_iota(jnp.int32, (8, 128), 0)
    index = lax.broadcasted_iota(jnp.int32, (8, 128), 1).astype(F32)
    o = jnp.where(index < total, o, float(ATOMS_DEV))
    out = jnp.where(row == 0, t, jnp.where(row == 1, d, jnp.where(row == 2, o, total)))
    return out.astype(jnp.int32)


def exchange_kernel(
    na, ne, green, pack, meta,
    data, kron, terms,
    left_cc, right_cc, pack_n, meta_n, hl, hr, rc, rh, to_r, to_l, forward, shifts, tables, spread, send, recv,
):
    p = lax.axis_index("atom")
    q = lax.axis_index("energy")
    up, down = p < na - 1, p > 0
    right, left = q < ne - 1, q > 0
    where_to = {(0, 1): right, (0, -1): left, (1, 0): up, (-1, 0): down}

    def peer(da, de):
        return {"atom": p + da, "energy": q + de}

    barrier = pltpu.get_barrier_semaphore()
    for (da, de), there in where_to.items():
        @pl.when(there)
        def _(da=da, de=de):
            pl.semaphore_signal(barrier, inc=1, device_id=peer(da, de), device_id_type=MESH)

    low = lax.broadcasted_iota(jnp.int32, (2 * SQ, E_DEV), 1) < 64

    def mix(a, b):
        return jnp.where(low, a, b).astype(BF16)

    def far_atom(c):
        return c + 6 if c < 2 else c + 2

    for c in range(4):
        near = green[c].astype(F32)
        far = pltpu.roll(green[far_atom(c)].astype(F32), 64, 1)
        to_r[c] = mix(far, near)
        to_l[c] = mix(near, far)

    def clear(ref):
        ref[...] = jnp.zeros(ref.shape, ref.dtype)

    @pl.when(jnp.logical_not(left))
    def _():
        clear(hl)

    @pl.when(jnp.logical_not(right))
    def _():
        clear(hr)

    for side, there in ((0, down), (1, up)):
        @pl.when(jnp.logical_not(there))
        def _(side=side):
            clear(rc.at[pl.ds(2 * side, 2)])
            clear(rh.at[pl.ds(2 * side, 2)])
            clear(pack_n.at[side])
            clear(meta_n.at[side])

    slots = iter(range(16))

    def copy_to(source, target, da, de):
        i = next(slots)
        copy = pltpu.make_async_remote_copy(
            src_ref=source,
            dst_ref=target,
            send_sem=send.at[i],
            recv_sem=recv.at[i],
            device_id=peer(da, de),
            device_id_type=MESH,
        )
        return copy, where_to[da, de], where_to[-da, -de]

    def start(items):
        for copy, sends, _ in items:
            pl.when(sends)(copy.start)

    def arrive(items):
        for copy, _, gets in items:
            pl.when(gets)(copy.wait_recv)

    def sent(items):
        for copy, sends, _ in items:
            pl.when(sends)(copy.wait_send)

    halos = [
        [copy_to(to_r.at[c], hl.at[c], 0, 1), copy_to(to_l.at[c], hr.at[c], 0, -1)] for c in range(4)
    ]
    small = [
        copy_to(pack, pack_n.at[0], 1, 0),
        copy_to(pack, pack_n.at[1], -1, 0),
        copy_to(meta, meta_n.at[0], 1, 0),
        copy_to(meta, meta_n.at[1], -1, 0),
    ]
    rims = [
        copy_to(green.at[pl.ds(6, 2)], rc.at[pl.ds(0, 2)], 1, 0),
        copy_to(green.at[pl.ds(0, 2)], rc.at[pl.ds(2, 2)], -1, 0),
    ]
    passed = [
        copy_to(forward.at[pl.ds(0, 2)], rh.at[pl.ds(0, 2)], 1, 0),
        copy_to(forward.at[pl.ds(2, 2)], rh.at[pl.ds(2, 2)], -1, 0),
    ]

    pl.semaphore_wait(barrier, sum(there.astype(jnp.int32) for there in where_to.values()))
    start(halos[0])
    start(halos[1])
    start(small)
    start(rims)

    row = lax.broadcasted_iota(jnp.int32, (2 * E_DEV, E_DEV), 0)
    col = lax.broadcasted_iota(jnp.int32, (2 * E_DEV, E_DEV), 1)
    outer = row - E_DEV
    for kind in range(2):
        if kind == 0:
            energy = jnp.where(outer < 64, outer + 128, outer - 128)
        else:
            energy = jnp.where(outer < 64, outer - 64, outer + 64)
        delta = (jnp.where(row < E_DEV, row, energy) - col).astype(F32)
        for m in range(MODES):
            n, k = pack[SLOTS + m : SLOTS + m + 1, 0:1], pack[SLOTS + m : SLOTS + m + 1, 1:2]
            value = jnp.where(delta == -k, n, jnp.where(delta == k, n + 1.0, 0.0))
            shifts[kind, m // 2, :, (m % 2) * 128 : (m % 2) * 128 + 128] = value.astype(BF16)

    def expand(source, table, target):
        rows = jnp.concatenate(
            [source[0:SLOTS, m * SQ : (m + 1) * SQ] for m in range(MODES)], axis=0
        ).astype(BF16)
        wide = jnp.dot(rows, tables[table], preferred_element_type=F32)
        for m in range(MODES):
            for i in range(NORB):
                target[m, i * SLOTS : (i + 1) * SLOTS, :] = wide[
                    m * SLOTS : (m + 1) * SLOTS, i * 128 : (i + 1) * 128
                ]

    for group in range(4):
        left_cc[group, :, NORB * SLOTS :, :] = jnp.zeros((MODES, 256 - NORB * SLOTS, 128), F32)
    fill_tables(tables)
    spread[...] = spread_matrix()
    expand(pack, 0, left_cc.at[0])
    expand(pack, 1, right_cc.at[0])
    expand(pack, 2, left_cc.at[1])
    expand(pack, 3, right_cc.at[1])

    def build(group, s):
        for m in range(MODES):
            lanes = slice(m * 128, (m + 1) * 128)
            right = right_cc[group, m, pl.ds(s, 8, stride=SLOTS), :]
            left = left_cc[group, m, pl.ds(s, PADROW, stride=SLOTS), :]
            for i in range(0, NORB, 2):
                rows = [left_cc[group, m, pl.ds((i + n) * SLOTS + s, 1), :] * right for n in range(2)]
                kron[group * SLOTS + s, i * 8 : i * 8 + 16, lanes] = jnp.concatenate(rows, axis=0).astype(BF16)
            for l in range(8, NORB):
                row = right_cc[group, m, pl.ds(l * SLOTS + s, 1), :]
                at = NORB * 8 + (l - 8) * PADROW
                kron[group * SLOTS + s, at : at + PADROW, lanes] = (row * left).astype(BF16)

    def build_first(s, carry):
        build(0, s)
        return carry

    def build_second(s, carry):
        build(1, s)
        return carry

    def build_neighbours(s, carry):
        build(2, s)
        build(3, s)
        return carry

    lax.fori_loop(0, SLOTS, build_first, 0)
    sent(halos[0])
    start(halos[2])
    lax.fori_loop(0, SLOTS, build_second, 0)
    arrive(small)
    for side in range(2):
        expand(pack_n.at[side], 2, left_cc.at[2 + side])
        expand(pack_n.at[side], 3, right_cc.at[2 + side])

    heads = [meta[...], meta_n[0], meta_n[1]]
    terms[...] = term_list(*heads, (p * ATOMS_DEV).astype(F32))

    def shift(d, kind, centre, halo):
        wide = jnp.concatenate([centre, halo], axis=1)
        rows = jnp.dot(spread[...], wide, preferred_element_type=F32).astype(BF16)
        for pair in range(MODES // 2):
            both = jnp.dot(rows, shifts[kind, pair], preferred_element_type=F32).astype(BF16)
            for half in range(2):
                at = (2 * pair + half) * 128
                for part in range(2):
                    data[d, at : at + 128, part * 128 : part * 128 + 128] = both[
                        part * 128 : part * 128 + 128, half * 128 : half * 128 + 128
                    ]

    def own_halos(c):
        lower, upper = hl[c].astype(F32), hr[c].astype(F32)
        return mix(upper, lower), mix(lower, upper)

    def shift_own(c, far):
        near_halo, far_halo = own_halos(c)
        shift(c, 0, green[c], near_halo)
        shift(6 + c, 1, green[far], far_halo)

    sent(halos[1])
    start(halos[3])
    arrive(halos[0])
    arrive(halos[1])
    for c in range(2):
        near_halo, far_halo = own_halos(c)
        forward[c] = far_halo
        forward[2 + c] = near_halo
    start(passed)
    lax.fori_loop(0, SLOTS, build_neighbours, 0)

    def first_half(c, carry):
        shift_own(c, c + 6)
        return carry

    lax.fori_loop(0, 2, first_half, 0)
    arrive(halos[2])
    shift_own(2, 4)
    arrive(rims)
    arrive(passed)

    def rim(c, carry):
        shift(4 + c, 0, rc[2 + c], rh[2 + c])
        shift(10 + c, 1, rc[c], rh[c])
        return carry

    lax.fori_loop(0, 2, rim, 0)
    arrive(halos[3])
    shift_own(3, 5)
    for items in halos[2:] + [small, rims, passed]:
        sent(items)


def exchange(na, ne, green, pack, meta):
    vm = pl.BlockSpec(memory_space=pltpu.VMEM)
    slab = (2 * SQ, E_DEV)
    shape = jax.ShapeDtypeStruct
    return pl.pallas_call(
        functools.partial(exchange_kernel, na, ne),
        out_shape=[
            shape((ATOMS_DEV + 4, MODES * 128, 2 * E_DEV), BF16),
            shape((4 * SLOTS, KR, MODES * 128), BF16),
            shape((8, 128), jnp.int32),
        ],
        in_specs=[vm] * 3,
        out_specs=[vm] * 3,
        scratch_shapes=[
            pltpu.VMEM((4, MODES, 256, 128), F32),
            pltpu.VMEM((4, MODES, 256, 128), F32),
            pltpu.VMEM((2,) + pack.shape, F32),
            pltpu.VMEM((2,) + meta.shape, jnp.int32),
            pltpu.VMEM((4,) + slab, BF16),
            pltpu.VMEM((4,) + slab, BF16),
            pltpu.VMEM((4,) + slab, BF16),
            pltpu.VMEM((4,) + slab, BF16),
            pltpu.VMEM((4,) + slab, BF16),
            pltpu.VMEM((4,) + slab, BF16),
            pltpu.VMEM((4,) + slab, BF16),
            pltpu.VMEM((2, MODES // 2, 2 * E_DEV, 256), BF16),
            pltpu.VMEM((4, SQ, NORB * 128), BF16),
            pltpu.VMEM((256, 2 * SQ), BF16),
            pltpu.SemaphoreType.DMA((16,)),
            pltpu.SemaphoreType.DMA((16,)),
        ],
        compiler_params=pltpu.CompilerParams(
            collective_id=0, has_side_effects=True, vmem_limit_bytes=14 * 2**20
        ),
        name="exchange",
    )(green, pack, meta)


def born_kernel(terms, data, kron, out, acc, collect):
    total = terms[3, 0]
    acc[...] = jnp.zeros_like(acc)

    def visit(step, carry):
        for u in range(UNROLL):
            at = step * UNROLL + u
            t, d, o = terms[0, at], terms[1, at], terms[2, at]
            acc[o] += jnp.dot(kron[t], data[d], preferred_element_type=F32)
        return carry

    lax.fori_loop(0, lax.div(total + UNROLL - 1, UNROLL), visit, 0)

    collect[...] = collect_matrix()
    for o in range(0, ATOMS_DEV, 2):
        one, two = acc[o].astype(BF16), acc[o + 1].astype(BF16)
        tall = jnp.concatenate(
            [
                jnp.concatenate([one[:, :E_DEV], two[:, :E_DEV]], axis=1),
                jnp.concatenate([one[:, E_DEV:], two[:, E_DEV:]], axis=1),
            ],
            axis=0,
        )
        both = jnp.dot(collect[...], tall, preferred_element_type=F32).astype(BF16)
        out[o] = both[:, :E_DEV]
        out[o + 1] = both[:, E_DEV:]


def born(*arrays):
    vm = pl.BlockSpec(memory_space=pltpu.VMEM)
    return pl.pallas_call(
        born_kernel,
        out_shape=jax.ShapeDtypeStruct((ATOMS_DEV, 2 * SQ, E_DEV), BF16),
        in_specs=[pl.BlockSpec(memory_space=pltpu.SMEM)] + [vm] * 2,
        out_specs=vm,
        scratch_shapes=[
            pltpu.VMEM((ATOMS_DEV + 1, KR, 2 * E_DEV), F32),
            pltpu.VMEM((2 * SQ, 2 * KR), BF16),
        ],
        compiler_params=pltpu.CompilerParams(vmem_limit_bytes=6 * 2**20),
        name="born",
    )(*arrays)


def per_device(na, ne, green, coupling, pairs, counts, occupation, offsets):
    width = coupling.shape[1]
    lane = lax.broadcasted_iota(jnp.int32, (MODES, width), 1)
    modes = jnp.where(lane == 0, occupation[:, None], offsets.astype(F32)[:, None])
    pack = jnp.concatenate([coupling.astype(F32), modes], axis=0)
    meta = jnp.concatenate([pairs.T, jnp.broadcast_to(counts, (1, SLOTS))], axis=0)
    data, kron, terms = exchange(na, ne, green, pack, meta)
    return born(terms, data, kron)


def solution(mesh):
    placed = (P("atom", None, "energy"), P("atom", None), P("atom", None), P("atom"), P(), P())
    return jax.shard_map(
        functools.partial(per_device, mesh.shape["atom"], mesh.shape["energy"]),
        mesh=mesh,
        in_specs=placed,
        out_specs=P("atom", None, "energy"),
        check_vma=False,
    )
```

```python
import functools

import jax
import jax.numpy as jnp
from jax import lax
from jax.experimental import pallas as pl
from jax.experimental.pallas import tpu as pltpu
from jax.sharding import PartitionSpec as P

NORB = 10
MODES = 8
KMAX = 64
SQ = NORB * NORB
PADROW = 16
KR = NORB * 8 + 2 * PADROW
ATOMS_DEV = 8
E_DEV = 128
SLOTS = 16
MESH = pl.DeviceIdType.MESH
F32 = jnp.float32
BF16 = jnp.bfloat16
UNROLL = 4


def fill_tables(tables):
    row = lax.broadcasted_iota(jnp.int32, (SQ, 128), 0)
    lane = lax.broadcasted_iota(jnp.int32, (SQ, 128), 1)
    j = lax.shift_right_logical(lane * 205, 11)
    k = lane - j * NORB
    inside = lane < SQ
    for i in range(NORB):
        for table, want in enumerate((i * NORB + j, i * NORB + k, j * NORB + i, k * NORB + i)):
            tables[table, :, i * 128 : (i + 1) * 128] = one_where(inside & (row == want))


def one_where(mask):
    return jnp.where(mask, 1.0, 0.0).astype(BF16)


def spread_matrix():
    row = lax.broadcasted_iota(jnp.int32, (256, 2 * SQ), 0)
    col = lax.broadcasted_iota(jnp.int32, (256, 2 * SQ), 1)
    first = (row < SQ) & (col == row)
    second = (row >= 128) & (row < 128 + SQ) & (col == row - 128 + SQ)
    return one_where(first | second)


def collect_matrix():
    row = lax.broadcasted_iota(jnp.int32, (2 * SQ, 2 * KR), 0)
    col = lax.broadcasted_iota(jnp.int32, (2 * SQ, 2 * KR), 1)
    part = jnp.where(col < KR, 0, 1)
    at = col - part * KR
    late = at - NORB * 8
    early = late < 0
    i = jnp.where(early, lax.shift_right_logical(at, 3), late & (PADROW - 1))
    l = jnp.where(early, at & 7, 8 + lax.shift_right_logical(jnp.maximum(late, 0), 4))
    return one_where((i < NORB) & (row == part * SQ + i * NORB + l))


def term_list(own, below, above, base):
    lane = lax.broadcasted_iota(jnp.int32, (1, SLOTS), 1).astype(F32)

    def place(rel):
        inner = jnp.where((rel == 4) | (rel == 5), rel + 4, rel)
        return jnp.where(rel < 0, rel + 12, jnp.where(rel > 7, rel - 4, inner))

    entries = []
    for group, source in ((0, own), (2, below), (3, above)):
        a, b = source[0:1].astype(F32) - base, source[1:2].astype(F32) - base
        live = lane < source[2:3].astype(F32)
        if group == 0:
            entries.append((live, lane, place(b), a))
            group = 1
        entries.append((live & (b >= 0) & (b < 8), group * SLOTS + lane, place(a), b))

    before = one_where(
        lax.broadcasted_iota(jnp.int32, (SLOTS, SLOTS), 0) < lax.broadcasted_iota(jnp.int32, (SLOTS, SLOTS), 1)
    )
    place_at = lax.broadcasted_iota(jnp.int32, (128, SLOTS), 0).astype(F32)
    total = jnp.zeros((1, 1), F32)
    tables = [jnp.zeros((128, SLOTS), F32) for _ in range(3)]
    for keep, *values in entries:
        flags = jnp.where(keep, 1.0, 0.0)
        many = jnp.broadcast_to(flags, (8, SLOTS)).astype(BF16)
        at = jnp.dot(many, before, preferred_element_type=F32)[0:1] + total
        total = total + jnp.sum(flags, axis=1, keepdims=True)
        chosen = jnp.where(place_at == at, 1.0, 0.0) * flags
        tables = [table + chosen * value for table, value in zip(tables, values)]
    ones = jnp.ones((8, SLOTS), BF16)
    t, d, o = (
        lax.dot_general(ones, table.astype(BF16), (((1,), (1,)), ((), ())), preferred_element_type=F32)
        for table in tables
    )
    row = lax.broadcasted_iota(jnp.int32, (8, 128), 0)
    index = lax.broadcasted_iota(jnp.int32, (8, 128), 1).astype(F32)
    o = jnp.where(index < total, o, float(ATOMS_DEV))
    out = jnp.where(row == 0, t, jnp.where(row == 1, d, jnp.where(row == 2, o, total)))
    return out.astype(jnp.int32)


def exchange_kernel(
    na, ne, green, pack, meta,
    data, kron, terms,
    left_cc, right_cc, pack_n, meta_n, hl, hr, rc, rh, to_r, to_l, forward, shifts, tables, spread, send, recv,
):
    p = lax.axis_index("atom")
    q = lax.axis_index("energy")
    up, down = p < na - 1, p > 0
    right, left = q < ne - 1, q > 0
    where_to = {(0, 1): right, (0, -1): left, (1, 0): up, (-1, 0): down}

    def peer(da, de):
        return {"atom": p + da, "energy": q + de}

    barrier = pltpu.get_barrier_semaphore()
    for (da, de), there in where_to.items():
        @pl.when(there)
        def _(da=da, de=de):
            pl.semaphore_signal(barrier, inc=1, device_id=peer(da, de), device_id_type=MESH)

    low = lax.broadcasted_iota(jnp.int32, (2 * SQ, E_DEV), 1) < 64

    def mix(a, b):
        return jnp.where(low, a, b).astype(BF16)

    def far_atom(c):
        return c + 6 if c < 2 else c + 2

    for c in range(4):
        near = green[c].astype(F32)
        far = pltpu.roll(green[far_atom(c)].astype(F32), 64, 1)
        to_r[c] = mix(far, near)
        to_l[c] = mix(near, far)

    def clear(ref):
        ref[...] = jnp.zeros(ref.shape, ref.dtype)

    @pl.when(jnp.logical_not(left))
    def _():
        clear(hl)

    @pl.when(jnp.logical_not(right))
    def _():
        clear(hr)

    for side, there in ((0, down), (1, up)):
        @pl.when(jnp.logical_not(there))
        def _(side=side):
            clear(rc.at[pl.ds(2 * side, 2)])
            clear(rh.at[pl.ds(2 * side, 2)])
            clear(pack_n.at[side])
            clear(meta_n.at[side])

    slots = iter(range(16))

    def copy_to(source, target, da, de):
        i = next(slots)
        copy = pltpu.make_async_remote_copy(
            src_ref=source,
            dst_ref=target,
            send_sem=send.at[i],
            recv_sem=recv.at[i],
            device_id=peer(da, de),
            device_id_type=MESH,
        )
        return copy, where_to[da, de], where_to[-da, -de]

    def start(items):
        for copy, sends, _ in items:
            pl.when(sends)(copy.start)

    def arrive(items):
        for copy, _, gets in items:
            pl.when(gets)(copy.wait_recv)

    def sent(items):
        for copy, sends, _ in items:
            pl.when(sends)(copy.wait_send)

    halos = [
        [copy_to(to_r.at[c], hl.at[c], 0, 1), copy_to(to_l.at[c], hr.at[c], 0, -1)] for c in range(4)
    ]
    small = [
        copy_to(pack, pack_n.at[0], 1, 0),
        copy_to(pack, pack_n.at[1], -1, 0),
        copy_to(meta, meta_n.at[0], 1, 0),
        copy_to(meta, meta_n.at[1], -1, 0),
    ]
    rims = [
        copy_to(green.at[pl.ds(6, 2)], rc.at[pl.ds(0, 2)], 1, 0),
        copy_to(green.at[pl.ds(0, 2)], rc.at[pl.ds(2, 2)], -1, 0),
    ]
    passed = [
        copy_to(forward.at[pl.ds(0, 2)], rh.at[pl.ds(0, 2)], 1, 0),
        copy_to(forward.at[pl.ds(2, 2)], rh.at[pl.ds(2, 2)], -1, 0),
    ]

    pl.semaphore_wait(barrier, sum(there.astype(jnp.int32) for there in where_to.values()))
    start(halos[0])
    start(halos[1])
    start(small)
    start(rims)
    start(halos[2])
    start(halos[3])

    row = lax.broadcasted_iota(jnp.int32, (2 * E_DEV, E_DEV), 0)
    col = lax.broadcasted_iota(jnp.int32, (2 * E_DEV, E_DEV), 1)
    outer = row - E_DEV
    for kind in range(2):
        if kind == 0:
            energy = jnp.where(outer < 64, outer + 128, outer - 128)
        else:
            energy = jnp.where(outer < 64, outer - 64, outer + 64)
        delta = (jnp.where(row < E_DEV, row, energy) - col).astype(F32)
        for m in range(MODES):
            n, k = pack[SLOTS + m : SLOTS + m + 1, 0:1], pack[SLOTS + m : SLOTS + m + 1, 1:2]
            value = jnp.where(delta == -k, n, jnp.where(delta == k, n + 1.0, 0.0))
            shifts[kind, m // 2, :, (m % 2) * 128 : (m % 2) * 128 + 128] = value.astype(BF16)

    def expand(source, table, target):
        rows = jnp.concatenate(
            [source[0:SLOTS, m * SQ : (m + 1) * SQ] for m in range(MODES)], axis=0
        ).astype(BF16)
        wide = jnp.dot(rows, tables[table], preferred_element_type=F32)
        for m in range(MODES):
            for i in range(NORB):
                target[m, i * SLOTS : (i + 1) * SLOTS, :] = wide[
                    m * SLOTS : (m + 1) * SLOTS, i * 128 : (i + 1) * 128
                ]

    for group in range(4):
        left_cc[group, :, NORB * SLOTS :, :] = jnp.zeros((MODES, 256 - NORB * SLOTS, 128), F32)
    fill_tables(tables)
    spread[...] = spread_matrix()
    expand(pack, 0, left_cc.at[0])
    expand(pack, 1, right_cc.at[0])
    expand(pack, 2, left_cc.at[1])
    expand(pack, 3, right_cc.at[1])

    def build(group, s):
        for m in range(MODES):
            lanes = slice(m * 128, (m + 1) * 128)
            right = right_cc[group, m, pl.ds(s, 8, stride=SLOTS), :]
            left = left_cc[group, m, pl.ds(s, PADROW, stride=SLOTS), :]
            for i in range(0, NORB, 2):
                rows = [left_cc[group, m, pl.ds((i + n) * SLOTS + s, 1), :] * right for n in range(2)]
                kron[group * SLOTS + s, i * 8 : i * 8 + 16, lanes] = jnp.concatenate(rows, axis=0).astype(BF16)
            for l in range(8, NORB):
                row = right_cc[group, m, pl.ds(l * SLOTS + s, 1), :]
                at = NORB * 8 + (l - 8) * PADROW
                kron[group * SLOTS + s, at : at + PADROW, lanes] = (row * left).astype(BF16)

    def build_first(s, carry):
        build(0, s)
        return carry

    def build_second(s, carry):
        build(1, s)
        return carry

    def build_neighbours(s, carry):
        build(2, s)
        build(3, s)
        return carry

    lax.fori_loop(0, SLOTS, build_first, 0)
    lax.fori_loop(0, SLOTS, build_second, 0)
    arrive(small)
    for side in range(2):
        expand(pack_n.at[side], 2, left_cc.at[2 + side])
        expand(pack_n.at[side], 3, right_cc.at[2 + side])

    heads = [meta[...], meta_n[0], meta_n[1]]
    terms[...] = term_list(*heads, (p * ATOMS_DEV).astype(F32))

    def shift(d, kind, centre, halo):
        wide = jnp.concatenate([centre, halo], axis=1)
        rows = jnp.dot(spread[...], wide, preferred_element_type=F32).astype(BF16)
        for pair in range(MODES // 2):
            both = jnp.dot(rows, shifts[kind, pair], preferred_element_type=F32).astype(BF16)
            for half in range(2):
                at = (2 * pair + half) * 128
                for part in range(2):
                    data[d, at : at + 128, part * 128 : part * 128 + 128] = both[
                        part * 128 : part * 128 + 128, half * 128 : half * 128 + 128
                    ]

    def own_halos(c):
        lower, upper = hl[c].astype(F32), hr[c].astype(F32)
        return mix(upper, lower), mix(lower, upper)

    def shift_own(c, far):
        near_halo, far_halo = own_halos(c)
        shift(c, 0, green[c], near_halo)
        shift(6 + c, 1, green[far], far_halo)

    arrive(halos[0])
    arrive(halos[1])
    for c in range(2):
        near_halo, far_halo = own_halos(c)
        forward[c] = far_halo
        forward[2 + c] = near_halo
    start(passed)
    lax.fori_loop(0, SLOTS, build_neighbours, 0)

    def first_half(c, carry):
        shift_own(c, c + 6)
        return carry

    lax.fori_loop(0, 2, first_half, 0)
    arrive(halos[2])
    shift_own(2, 4)
    arrive(rims)
    arrive(passed)

    def rim(c, carry):
        shift(4 + c, 0, rc[2 + c], rh[2 + c])
        shift(10 + c, 1, rc[c], rh[c])
        return carry

    lax.fori_loop(0, 2, rim, 0)
    arrive(halos[3])
    shift_own(3, 5)
    for items in halos + [small, rims, passed]:
        sent(items)


def exchange(na, ne, green, pack, meta):
    vm = pl.BlockSpec(memory_space=pltpu.VMEM)
    slab = (2 * SQ, E_DEV)
    shape = jax.ShapeDtypeStruct
    return pl.pallas_call(
        functools.partial(exchange_kernel, na, ne),
        out_shape=[
            shape((ATOMS_DEV + 4, MODES * 128, 2 * E_DEV), BF16),
            shape((4 * SLOTS, KR, MODES * 128), BF16),
            shape((8, 128), jnp.int32),
        ],
        in_specs=[vm] * 3,
        out_specs=[vm] * 3,
        scratch_shapes=[
            pltpu.VMEM((4, MODES, 256, 128), F32),
            pltpu.VMEM((4, MODES, 256, 128), F32),
            pltpu.VMEM((2,) + pack.shape, F32),
            pltpu.VMEM((2,) + meta.shape, jnp.int32),
            pltpu.VMEM((4,) + slab, BF16),
            pltpu.VMEM((4,) + slab, BF16),
            pltpu.VMEM((4,) + slab, BF16),
            pltpu.VMEM((4,) + slab, BF16),
            pltpu.VMEM((4,) + slab, BF16),
            pltpu.VMEM((4,) + slab, BF16),
            pltpu.VMEM((4,) + slab, BF16),
            pltpu.VMEM((2, MODES // 2, 2 * E_DEV, 256), BF16),
            pltpu.VMEM((4, SQ, NORB * 128), BF16),
            pltpu.VMEM((256, 2 * SQ), BF16),
            pltpu.SemaphoreType.DMA((16,)),
            pltpu.SemaphoreType.DMA((16,)),
        ],
        compiler_params=pltpu.CompilerParams(
            collective_id=0, has_side_effects=True, vmem_limit_bytes=14 * 2**20
        ),
        name="exchange",
    )(green, pack, meta)


def born_kernel(terms, data, kron, out, acc, collect):
    total = terms[3, 0]
    acc[...] = jnp.zeros_like(acc)

    def visit(step, carry):
        for u in range(UNROLL):
            at = step * UNROLL + u
            t, d, o = terms[0, at], terms[1, at], terms[2, at]
            acc[o] += jnp.dot(kron[t], data[d], preferred_element_type=F32)
        return carry

    lax.fori_loop(0, lax.div(total + UNROLL - 1, UNROLL), visit, 0)

    collect[...] = collect_matrix()
    for o in range(0, ATOMS_DEV, 2):
        one, two = acc[o].astype(BF16), acc[o + 1].astype(BF16)
        tall = jnp.concatenate(
            [
                jnp.concatenate([one[:, :E_DEV], two[:, :E_DEV]], axis=1),
                jnp.concatenate([one[:, E_DEV:], two[:, E_DEV:]], axis=1),
            ],
            axis=0,
        )
        both = jnp.dot(collect[...], tall, preferred_element_type=F32).astype(BF16)
        out[o] = both[:, :E_DEV]
        out[o + 1] = both[:, E_DEV:]


def born(*arrays):
    vm = pl.BlockSpec(memory_space=pltpu.VMEM)
    return pl.pallas_call(
        born_kernel,
        out_shape=jax.ShapeDtypeStruct((ATOMS_DEV, 2 * SQ, E_DEV), BF16),
        in_specs=[pl.BlockSpec(memory_space=pltpu.SMEM)] + [vm] * 2,
        out_specs=vm,
        scratch_shapes=[
            pltpu.VMEM((ATOMS_DEV + 1, KR, 2 * E_DEV), F32),
            pltpu.VMEM((2 * SQ, 2 * KR), BF16),
        ],
        compiler_params=pltpu.CompilerParams(vmem_limit_bytes=6 * 2**20),
        name="born",
    )(*arrays)


def per_device(na, ne, green, coupling, pairs, counts, occupation, offsets):
    width = coupling.shape[1]
    lane = lax.broadcasted_iota(jnp.int32, (MODES, width), 1)
    modes = jnp.where(lane == 0, occupation[:, None], offsets.astype(F32)[:, None])
    pack = jnp.concatenate([coupling.astype(F32), modes], axis=0)
    meta = jnp.concatenate([pairs.T, jnp.broadcast_to(counts, (1, SLOTS))], axis=0)
    data, kron, terms = exchange(na, ne, green, pack, meta)
    return born(terms, data, kron)


def solution(mesh):
    placed = (P("atom", None, "energy"), P("atom", None), P("atom", None), P("atom"), P(), P())
    return jax.shard_map(
        functools.partial(per_device, mesh.shape["atom"], mesh.shape["energy"]),
        mesh=mesh,
        in_specs=placed,
        out_specs=P("atom", None, "energy"),
        check_vma=False,
    )
```

```python
import functools

import jax
import jax.numpy as jnp
from jax import lax
from jax.experimental import pallas as pl
from jax.experimental.pallas import tpu as pltpu
from jax.sharding import PartitionSpec as P

NORB = 10
MODES = 8
KMAX = 64
SQ = NORB * NORB
PADROW = 16
KR = NORB * 8 + 2 * PADROW
ATOMS_DEV = 8
E_DEV = 128
SLOTS = 16
MESH = pl.DeviceIdType.MESH
F32 = jnp.float32
BF16 = jnp.bfloat16
UNROLL = 4


def fill_tables(tables):
    row = lax.broadcasted_iota(jnp.int32, (SQ, 128), 0)
    lane = lax.broadcasted_iota(jnp.int32, (SQ, 128), 1)
    j = lax.shift_right_logical(lane * 205, 11)
    k = lane - j * NORB
    inside = lane < SQ
    for i in range(NORB):
        for table, want in enumerate((i * NORB + j, i * NORB + k, j * NORB + i, k * NORB + i)):
            tables[table, :, i * 128 : (i + 1) * 128] = one_where(inside & (row == want))


def one_where(mask):
    return jnp.where(mask, 1.0, 0.0).astype(BF16)


def spread_matrix():
    row = lax.broadcasted_iota(jnp.int32, (256, 2 * SQ), 0)
    col = lax.broadcasted_iota(jnp.int32, (256, 2 * SQ), 1)
    first = (row < SQ) & (col == row)
    second = (row >= 128) & (row < 128 + SQ) & (col == row - 128 + SQ)
    return one_where(first | second)


def collect_matrix():
    row = lax.broadcasted_iota(jnp.int32, (2 * SQ, 2 * KR), 0)
    col = lax.broadcasted_iota(jnp.int32, (2 * SQ, 2 * KR), 1)
    part = jnp.where(col < KR, 0, 1)
    at = col - part * KR
    late = at - NORB * 8
    early = late < 0
    i = jnp.where(early, lax.shift_right_logical(at, 3), late & (PADROW - 1))
    l = jnp.where(early, at & 7, 8 + lax.shift_right_logical(jnp.maximum(late, 0), 4))
    return one_where((i < NORB) & (row == part * SQ + i * NORB + l))


def term_list(own, below, above, base):
    lane = lax.broadcasted_iota(jnp.int32, (1, SLOTS), 1).astype(F32)

    def place(rel):
        inner = jnp.where((rel == 4) | (rel == 5), rel + 4, rel)
        return jnp.where(rel < 0, rel + 12, jnp.where(rel > 7, rel - 4, inner))

    entries = []
    for group, source in ((0, own), (2, below), (3, above)):
        a, b = source[0:1].astype(F32) - base, source[1:2].astype(F32) - base
        live = lane < source[2:3].astype(F32)
        if group == 0:
            entries.append((live, lane, place(b), a))
            group = 1
        entries.append((live & (b >= 0) & (b < 8), group * SLOTS + lane, place(a), b))

    before = one_where(
        lax.broadcasted_iota(jnp.int32, (SLOTS, SLOTS), 0) < lax.broadcasted_iota(jnp.int32, (SLOTS, SLOTS), 1)
    )
    place_at = lax.broadcasted_iota(jnp.int32, (128, SLOTS), 0).astype(F32)
    total = jnp.zeros((1, 1), F32)
    tables = [jnp.zeros((128, SLOTS), F32) for _ in range(3)]
    for keep, *values in entries:
        flags = jnp.where(keep, 1.0, 0.0)
        many = jnp.broadcast_to(flags, (8, SLOTS)).astype(BF16)
        at = jnp.dot(many, before, preferred_element_type=F32)[0:1] + total
        total = total + jnp.sum(flags, axis=1, keepdims=True)
        chosen = jnp.where(place_at == at, 1.0, 0.0) * flags
        tables = [table + chosen * value for table, value in zip(tables, values)]
    ones = jnp.ones((8, SLOTS), BF16)
    t, d, o = (
        lax.dot_general(ones, table.astype(BF16), (((1,), (1,)), ((), ())), preferred_element_type=F32)
        for table in tables
    )
    row = lax.broadcasted_iota(jnp.int32, (8, 128), 0)
    index = lax.broadcasted_iota(jnp.int32, (8, 128), 1).astype(F32)
    o = jnp.where(index < total, o, float(ATOMS_DEV))
    out = jnp.where(row == 0, t, jnp.where(row == 1, d, jnp.where(row == 2, o, total)))
    return out.astype(jnp.int32)


def exchange_kernel(
    na, ne, green, pack, meta,
    data, kron, terms,
    left_cc, right_cc, pack_n, meta_n, hl, hr, rc, rh, to_r, to_l, forward, shifts, tables, spread, send, recv,
):
    p = lax.axis_index("atom")
    q = lax.axis_index("energy")
    up, down = p < na - 1, p > 0
    right, left = q < ne - 1, q > 0
    where_to = {(0, 1): right, (0, -1): left, (1, 0): up, (-1, 0): down}

    def peer(da, de):
        return {"atom": p + da, "energy": q + de}

    barrier = pltpu.get_barrier_semaphore()
    for (da, de), there in where_to.items():
        @pl.when(there)
        def _(da=da, de=de):
            pl.semaphore_signal(barrier, inc=1, device_id=peer(da, de), device_id_type=MESH)

    low = lax.broadcasted_iota(jnp.int32, (2 * SQ, E_DEV), 1) < 64

    def mix(a, b):
        return jnp.where(low, a, b).astype(BF16)

    def far_atom(c):
        return c + 6 if c < 2 else c + 2

    for c in range(4):
        near = green[c].astype(F32)
        far = pltpu.roll(green[far_atom(c)].astype(F32), 64, 1)
        to_r[c] = mix(far, near)
        to_l[c] = mix(near, far)

    def clear(ref):
        ref[...] = jnp.zeros(ref.shape, ref.dtype)

    @pl.when(jnp.logical_not(left))
    def _():
        clear(hl)

    @pl.when(jnp.logical_not(right))
    def _():
        clear(hr)

    for side, there in ((0, down), (1, up)):
        @pl.when(jnp.logical_not(there))
        def _(side=side):
            clear(rc.at[pl.ds(2 * side, 2)])
            clear(rh.at[pl.ds(2 * side, 2)])
            clear(pack_n.at[side])
            clear(meta_n.at[side])

    slots = iter(range(16))

    def copy_to(source, target, da, de):
        i = next(slots)
        copy = pltpu.make_async_remote_copy(
            src_ref=source,
            dst_ref=target,
            send_sem=send.at[i],
            recv_sem=recv.at[i],
            device_id=peer(da, de),
            device_id_type=MESH,
        )
        return copy, where_to[da, de], where_to[-da, -de]

    def start(items):
        for copy, sends, _ in items:
            pl.when(sends)(copy.start)

    def arrive(items):
        for copy, _, gets in items:
            pl.when(gets)(copy.wait_recv)

    def sent(items):
        for copy, sends, _ in items:
            pl.when(sends)(copy.wait_send)

    halos = [
        [copy_to(to_r.at[c], hl.at[c], 0, 1), copy_to(to_l.at[c], hr.at[c], 0, -1)] for c in range(4)
    ]
    small = [
        copy_to(pack, pack_n.at[0], 1, 0),
        copy_to(pack, pack_n.at[1], -1, 0),
        copy_to(meta, meta_n.at[0], 1, 0),
        copy_to(meta, meta_n.at[1], -1, 0),
    ]
    rims = [
        copy_to(green.at[pl.ds(6, 2)], rc.at[pl.ds(0, 2)], 1, 0),
        copy_to(green.at[pl.ds(0, 2)], rc.at[pl.ds(2, 2)], -1, 0),
    ]
    passed = [
        copy_to(forward.at[pl.ds(0, 2)], rh.at[pl.ds(0, 2)], 1, 0),
        copy_to(forward.at[pl.ds(2, 2)], rh.at[pl.ds(2, 2)], -1, 0),
    ]

    pl.semaphore_wait(barrier, sum(there.astype(jnp.int32) for there in where_to.values()))
    start(halos[0])
    start(halos[1])
    start(small)
    start(rims)
    start(halos[2])
    start(halos[3])

    row = lax.broadcasted_iota(jnp.int32, (2 * E_DEV, E_DEV), 0)
    col = lax.broadcasted_iota(jnp.int32, (2 * E_DEV, E_DEV), 1)
    outer = row - E_DEV
    for kind in range(2):
        if kind == 0:
            energy = jnp.where(outer < 64, outer + 128, outer - 128)
        else:
            energy = jnp.where(outer < 64, outer - 64, outer + 64)
        delta = (jnp.where(row < E_DEV, row, energy) - col).astype(F32)
        for m in range(MODES):
            n, k = pack[SLOTS + m : SLOTS + m + 1, 0:1], pack[SLOTS + m : SLOTS + m + 1, 1:2]
            value = jnp.where(delta == -k, n, jnp.where(delta == k, n + 1.0, 0.0))
            shifts[kind, m // 2, :, (m % 2) * 128 : (m % 2) * 128 + 128] = value.astype(BF16)

    def expand(source, table, target):
        rows = jnp.concatenate(
            [source[0:SLOTS, m * SQ : (m + 1) * SQ] for m in range(MODES)], axis=0
        ).astype(BF16)
        wide = jnp.dot(rows, tables[table], preferred_element_type=F32)
        for m in range(MODES):
            for i in range(NORB):
                target[m, i * SLOTS : (i + 1) * SLOTS, :] = wide[
                    m * SLOTS : (m + 1) * SLOTS, i * 128 : (i + 1) * 128
                ]

    for group in range(4):
        left_cc[group, :, NORB * SLOTS :, :] = jnp.zeros((MODES, 256 - NORB * SLOTS, 128), F32)
    fill_tables(tables)
    spread[...] = spread_matrix()
    expand(pack, 0, left_cc.at[0])
    expand(pack, 1, right_cc.at[0])
    expand(pack, 2, left_cc.at[1])
    expand(pack, 3, right_cc.at[1])

    def build(group, s):
        for m in range(MODES):
            lanes = slice(m * 128, (m + 1) * 128)
            right = right_cc[group, m, pl.ds(s, 8, stride=SLOTS), :]
            left = left_cc[group, m, pl.ds(s, PADROW, stride=SLOTS), :]
            for i in range(0, NORB, 2):
                rows = [left_cc[group, m, pl.ds((i + n) * SLOTS + s, 1), :] * right for n in range(2)]
                kron[group * SLOTS + s, i * 8 : i * 8 + 16, lanes] = jnp.concatenate(rows, axis=0).astype(BF16)
            for l in range(8, NORB):
                row = right_cc[group, m, pl.ds(l * SLOTS + s, 1), :]
                at = NORB * 8 + (l - 8) * PADROW
                kron[group * SLOTS + s, at : at + PADROW, lanes] = (row * left).astype(BF16)

    def build_first(s, carry):
        build(0, s)
        return carry

    def build_second(s, carry):
        build(1, s)
        return carry

    def build_neighbours(s, carry):
        build(2, s)
        build(3, s)
        return carry

    lax.fori_loop(0, SLOTS, build_first, 0)
    def own_halos(c):
        lower, upper = hl[c].astype(F32), hr[c].astype(F32)
        return mix(upper, lower), mix(lower, upper)

    arrive(halos[0])
    arrive(halos[1])
    for c in range(2):
        near_halo, far_halo = own_halos(c)
        forward[c] = far_halo
        forward[2 + c] = near_halo
    start(passed)
    lax.fori_loop(0, SLOTS, build_second, 0)
    arrive(small)
    for side in range(2):
        expand(pack_n.at[side], 2, left_cc.at[2 + side])
        expand(pack_n.at[side], 3, right_cc.at[2 + side])

    heads = [meta[...], meta_n[0], meta_n[1]]
    terms[...] = term_list(*heads, (p * ATOMS_DEV).astype(F32))

    def shift(d, kind, centre, halo):
        wide = jnp.concatenate([centre, halo], axis=1)
        rows = jnp.dot(spread[...], wide, preferred_element_type=F32).astype(BF16)
        for pair in range(MODES // 2):
            both = jnp.dot(rows, shifts[kind, pair], preferred_element_type=F32).astype(BF16)
            for half in range(2):
                at = (2 * pair + half) * 128
                for part in range(2):
                    data[d, at : at + 128, part * 128 : part * 128 + 128] = both[
                        part * 128 : part * 128 + 128, half * 128 : half * 128 + 128
                    ]

    def shift_own(c, far):
        near_halo, far_halo = own_halos(c)
        shift(c, 0, green[c], near_halo)
        shift(6 + c, 1, green[far], far_halo)

    lax.fori_loop(0, SLOTS, build_neighbours, 0)

    def first_half(c, carry):
        shift_own(c, c + 6)
        return carry

    lax.fori_loop(0, 2, first_half, 0)
    arrive(halos[2])
    shift_own(2, 4)
    arrive(rims)
    arrive(passed)

    def rim(c, carry):
        shift(4 + c, 0, rc[2 + c], rh[2 + c])
        shift(10 + c, 1, rc[c], rh[c])
        return carry

    lax.fori_loop(0, 2, rim, 0)
    arrive(halos[3])
    shift_own(3, 5)
    for items in halos + [small, rims, passed]:
        sent(items)


def exchange(na, ne, green, pack, meta):
    vm = pl.BlockSpec(memory_space=pltpu.VMEM)
    slab = (2 * SQ, E_DEV)
    shape = jax.ShapeDtypeStruct
    return pl.pallas_call(
        functools.partial(exchange_kernel, na, ne),
        out_shape=[
            shape((ATOMS_DEV + 4, MODES * 128, 2 * E_DEV), BF16),
            shape((4 * SLOTS, KR, MODES * 128), BF16),
            shape((8, 128), jnp.int32),
        ],
        in_specs=[vm] * 3,
        out_specs=[vm] * 3,
        scratch_shapes=[
            pltpu.VMEM((4, MODES, 256, 128), F32),
            pltpu.VMEM((4, MODES, 256, 128), F32),
            pltpu.VMEM((2,) + pack.shape, F32),
            pltpu.VMEM((2,) + meta.shape, jnp.int32),
            pltpu.VMEM((4,) + slab, BF16),
            pltpu.VMEM((4,) + slab, BF16),
            pltpu.VMEM((4,) + slab, BF16),
            pltpu.VMEM((4,) + slab, BF16),
            pltpu.VMEM((4,) + slab, BF16),
            pltpu.VMEM((4,) + slab, BF16),
            pltpu.VMEM((4,) + slab, BF16),
            pltpu.VMEM((2, MODES // 2, 2 * E_DEV, 256), BF16),
            pltpu.VMEM((4, SQ, NORB * 128), BF16),
            pltpu.VMEM((256, 2 * SQ), BF16),
            pltpu.SemaphoreType.DMA((16,)),
            pltpu.SemaphoreType.DMA((16,)),
        ],
        compiler_params=pltpu.CompilerParams(
            collective_id=0, has_side_effects=True, vmem_limit_bytes=14 * 2**20
        ),
        name="exchange",
    )(green, pack, meta)


def born_kernel(terms, data, kron, out, acc, collect):
    total = terms[3, 0]
    acc[...] = jnp.zeros_like(acc)

    def visit(step, carry):
        for u in range(UNROLL):
            at = step * UNROLL + u
            t, d, o = terms[0, at], terms[1, at], terms[2, at]
            acc[o] += jnp.dot(kron[t], data[d], preferred_element_type=F32)
        return carry

    lax.fori_loop(0, lax.div(total + UNROLL - 1, UNROLL), visit, 0)

    collect[...] = collect_matrix()
    for o in range(0, ATOMS_DEV, 2):
        one, two = acc[o].astype(BF16), acc[o + 1].astype(BF16)
        tall = jnp.concatenate(
            [
                jnp.concatenate([one[:, :E_DEV], two[:, :E_DEV]], axis=1),
                jnp.concatenate([one[:, E_DEV:], two[:, E_DEV:]], axis=1),
            ],
            axis=0,
        )
        both = jnp.dot(collect[...], tall, preferred_element_type=F32).astype(BF16)
        out[o] = both[:, :E_DEV]
        out[o + 1] = both[:, E_DEV:]


def born(*arrays):
    vm = pl.BlockSpec(memory_space=pltpu.VMEM)
    return pl.pallas_call(
        born_kernel,
        out_shape=jax.ShapeDtypeStruct((ATOMS_DEV, 2 * SQ, E_DEV), BF16),
        in_specs=[pl.BlockSpec(memory_space=pltpu.SMEM)] + [vm] * 2,
        out_specs=vm,
        scratch_shapes=[
            pltpu.VMEM((ATOMS_DEV + 1, KR, 2 * E_DEV), F32),
            pltpu.VMEM((2 * SQ, 2 * KR), BF16),
        ],
        compiler_params=pltpu.CompilerParams(vmem_limit_bytes=6 * 2**20),
        name="born",
    )(*arrays)


def per_device(na, ne, green, coupling, pairs, counts, occupation, offsets):
    width = coupling.shape[1]
    lane = lax.broadcasted_iota(jnp.int32, (MODES, width), 1)
    modes = jnp.where(lane == 0, occupation[:, None], offsets.astype(F32)[:, None])
    pack = jnp.concatenate([coupling.astype(F32), modes], axis=0)
    meta = jnp.concatenate([pairs.T, jnp.broadcast_to(counts, (1, SLOTS))], axis=0)
    data, kron, terms = exchange(na, ne, green, pack, meta)
    return born(terms, data, kron)


def solution(mesh):
    placed = (P("atom", None, "energy"), P("atom", None), P("atom", None), P("atom"), P(), P())
    return jax.shard_map(
        functools.partial(per_device, mesh.shape["atom"], mesh.shape["energy"]),
        mesh=mesh,
        in_specs=placed,
        out_specs=P("atom", None, "energy"),
        check_vma=False,
    )
```
